512 devices in a mesh: hid: 32 (over z, y_lo), wid: 16 (over y_hi, x, core).
Axes of the slice: x: 4, y: 4 (y_hi: 2, y_lo: 2; y = y_hi * 2 + y_lo), z: 16, core: 2. Of those that a mesh axis runs over, the one named last changes fastest.
Arguments:
- inputs: bfloat16 [512, 6144], P('hid', 'wid'), may hold values from -420 to 420
- cotangent: bfloat16 [512, 6144], P('hid', 'wid'), may hold values from -6 to 6
- norm_gain: float32 [6144], P('wid'), may hold values from 0.5 to 1.5
- qkv_weight: bfloat16 [6144, 3, 4096], P('wid', None, 'hid'), may hold values from -0.078125 to 0.078125
- out_weight: bfloat16 [4096, 6144], P('hid', 'wid'), may hold values from -0.375 to 0.375
- up_weight: bfloat16 [6144, 16384], P('wid', 'hid'), may hold values from -0.078125 to 0.078125
- down_weight: bfloat16 [16384, 6144], P('hid', 'wid'), may hold values from -0.046875 to 0.046875
- query_gain: float32 [128], replicated, may hold values from 0.5 to 1.5
- key_gain: float32 [128], replicated, may hold values from 0.5 to 1.5
Outputs:
- input_grad: bfloat16 [512, 6144], P('hid', 'wid')
- qkv_grad: bfloat16 [6144, 3, 4096], P('wid', None, 'hid')
- out_grad: bfloat16 [4096, 6144], P('hid', 'wid')
- up_grad: bfloat16 [6144, 16384], P('wid', 'hid')
- down_grad: bfloat16 [16384, 6144], P('hid', 'wid')
The draws below stay inside these ranges and needn't reach their ends.
All inputs are finite; a program needn't handle non-finite values.
Results may differ from the reference program's by a relative error of at most 0.011.
Values may be sent and summed in bfloat16 or wider, within the bound.
No kernel may reach another device: no remote copies, remote signals or barrier semaphores. Data moves between devices by JAX's collectives and lax.ppermute only.
A program may use at most 64 MiB of HBM per device.

```python
import math
import jax
import jax.numpy as jnp
from jax import lax

D = 6144
FF = 16384
HEADS = 32
HEAD_DIM = 128
PATCHES = 256
TOKENS = 512


def draw_inputs(key, part):
    key = jax.random.fold_in(key, 11)
    column_key, row_key, base_key = jax.random.split(key, 3)
    rise = math.log10(3.0)
    column_ramp = jnp.arange(D, dtype=jnp.float32) / (D - 1) * rise
    column_scale = 10.0 ** (jax.random.uniform(column_key, (D,), jnp.float32) * (1.0 - rise) + column_ramp)
    row_scale = 10.0 ** jax.random.uniform(row_key, (TOKENS, 1), jnp.float32)
    base_values = jnp.clip(jax.random.normal(base_key, (TOKENS, D), jnp.float32), -4.0, 4.0)
    values = row_scale * column_scale * base_values
    return values.astype(jnp.bfloat16)


def level_of(stream_key, dims, cuts, smallest, high):
    def one(axis_at, blocks):
        draws = jax.random.uniform(jax.random.fold_in(jax.random.fold_in(stream_key, 6), axis_at), (blocks,), jnp.float32, smallest / len(cuts), high / len(cuts))
        return jnp.repeat(jnp.exp(draws), dims[axis_at] // blocks).reshape((-1,) + (1,) * (len(dims) - axis_at - 1))

    level = one(*cuts[0])
    for cut in cuts[1:]:
        level = level * one(*cut)
    return level


def bell_draw(own_key, extent, spread, limit, pieces=(), kind=jnp.bfloat16):
    array = jax.random.normal(own_key, extent, jnp.float32) * spread
    if len(pieces) > 0:
        array = level_of(own_key, extent, pieces, -0.22, 0.18) * array
    return jnp.clip(array, min=-limit, max=limit).astype(kind)


def setup_inputs(seed: int = 0) -> dict:
    keys = jax.random.split(jax.random.key(seed), 10)
    return {
        "inputs": draw_inputs(jax.random.fold_in(keys[9], 71), 0),
        "cotangent": bell_draw(keys[1], (TOKENS, D), 1.0, 6.0, ((0, 32), (1, 16))),
        "norm_gain": jnp.clip(1.0 + 0.1 * jax.random.normal(keys[2], (D,), jnp.float32), 0.5, 1.5),
        "qkv_weight": bell_draw(keys[3], (D, 3, HEADS * HEAD_DIM), D ** -0.5, 0.078125, ((0, 16), (2, 32))),
        "out_weight": bell_draw(keys[4], (HEADS * HEAD_DIM, D), (HEADS * HEAD_DIM // 16) ** -0.5, 0.375, ((0, 32), (1, 16))),
        "up_weight": bell_draw(keys[5], (D, FF), D ** -0.5, 0.078125, ((0, 16), (1, 32))),
        "down_weight": bell_draw(keys[6], (FF, D), FF ** -0.5, 0.046875, ((0, 32), (1, 16))),
        "query_gain": jnp.clip(1.0 + 0.1 * jax.random.normal(keys[7], (HEAD_DIM,), jnp.float32), 0.5, 1.5),
        "key_gain": jnp.clip(1.0 + 0.1 * jax.random.normal(keys[8], (HEAD_DIM,), jnp.float32), 0.5, 1.5),
    }


EPSILON = 1e-06

def product(form, left_arr, right_arr):
    return jnp.einsum(form, left_arr.astype(jnp.float32), right_arr.astype(jnp.float32))

def head_norm(values, gain):
    centre = lax.optimization_barrier(jnp.mean(values, axis=-1, keepdims=True))
    centred = values - centre
    inverse = lax.rsqrt(lax.optimization_barrier(jnp.mean(centred * centred, axis=-1, keepdims=True)) + EPSILON)
    unit_rows = centred * inverse
    return (unit_rows, inverse, unit_rows * gain)

def head_norm_back(upstream, unit_rows, inverse, gain):
    scaled = upstream * gain
    return inverse * (scaled - lax.optimization_barrier(jnp.mean(scaled, axis=-1, keepdims=True)) - unit_rows * lax.optimization_barrier(jnp.mean(scaled * unit_rows, axis=-1, keepdims=True)))

def gelu_pair(pre_act, upstream):
    hidden, pullback = jax.vjp(jax.nn.gelu, pre_act)
    return (hidden.astype(jnp.bfloat16), pullback(upstream)[0].astype(jnp.bfloat16))

def attention_pair(qkv_rows, att_grad, query_gain, key_gain):
    tok_count = qkv_rows.shape[0]
    head_width = qkv_rows.shape[2]
    head_count = head_width // HEAD_DIM
    image_count = tok_count // PATCHES
    score_scale = 1.0 / math.sqrt(HEAD_DIM)

    def per_image(values):
        return values.reshape(image_count, PATCHES, head_count, HEAD_DIM)
    query_unit, query_inverse, query_normed = head_norm(per_image(qkv_rows[:, 0]), query_gain)
    key_unit, key_inverse, key_normed = head_norm(per_image(qkv_rows[:, 1]), key_gain)
    query_normed = query_normed.astype(jnp.bfloat16)
    key_normed = key_normed.astype(jnp.bfloat16)
    value_rows = per_image(qkv_rows[:, 2]).astype(jnp.bfloat16)
    scores = product('ipha,iqha->ihpq', query_normed, key_normed) * score_scale
    exponent = jnp.exp(scores)
    probs = exponent / lax.optimization_barrier(jnp.sum(exponent, axis=-1, keepdims=True))
    probs_low = probs.astype(jnp.bfloat16)
    attended = product('ihpq,iqha->ipha', probs_low, value_rows).astype(jnp.bfloat16).reshape(tok_count, head_width)
    grad_rows = per_image(att_grad)
    probs_grad = product('ipha,iqha->ihpq', grad_rows, value_rows)
    value_grad = product('ihpq,ipha->iqha', probs_low, grad_rows)
    score_grad = (probs * (probs_grad - lax.optimization_barrier(jnp.sum(probs * probs_grad, axis=-1, keepdims=True))) * score_scale).astype(jnp.bfloat16)
    qn_grad = product('ihpq,iqha->ipha', score_grad, key_normed)
    kn_grad = product('ihpq,ipha->iqha', score_grad, query_normed)
    query_grad = head_norm_back(qn_grad, query_unit, query_inverse, query_gain)
    key_grad = head_norm_back(kn_grad, key_unit, key_inverse, key_gain)
    qkv_back = jnp.stack([query_grad.reshape(tok_count, head_width), key_grad.reshape(tok_count, head_width), value_grad.reshape(tok_count, head_width)], axis=1).astype(jnp.bfloat16)
    return (attended, qkv_back)

def reference(inputs, cotangent, norm_gain, qkv_weight, out_weight, up_weight, down_weight, query_gain, key_gain):
    input_rows = inputs.astype(jnp.float32)
    centre = lax.optimization_barrier(jnp.mean(input_rows, axis=-1, keepdims=True))
    centred = input_rows - centre
    inverse = lax.rsqrt(lax.optimization_barrier(jnp.mean(centred * centred, axis=-1, keepdims=True)) + EPSILON)
    unit_rows = centred * inverse
    normed = (unit_rows * norm_gain).astype(jnp.bfloat16)
    pre_act = jnp.dot(normed, up_weight, preferred_element_type=jnp.float32)
    qkv_rows = product('td,dch->tch', normed, qkv_weight)
    hidden_grad = jnp.dot(cotangent, down_weight.T, preferred_element_type=jnp.float32)
    att_grad = jnp.dot(cotangent, out_weight.T, preferred_element_type=jnp.float32).astype(jnp.bfloat16)
    hidden, pre_grad = gelu_pair(pre_act, hidden_grad)
    attended, qkv_back = attention_pair(qkv_rows, att_grad, query_gain, key_gain)
    qkv_grad = product('td,tch->dch', normed, qkv_back).astype(jnp.bfloat16)
    out_grad = jnp.dot(attended.T, cotangent, preferred_element_type=jnp.float32).astype(jnp.bfloat16)
    up_grad = jnp.dot(normed.T, pre_grad, preferred_element_type=jnp.float32).astype(jnp.bfloat16)
    down_grad = jnp.dot(hidden.T, cotangent, preferred_element_type=jnp.float32).astype(jnp.bfloat16)
    normed_grad = jnp.dot(pre_grad, up_weight.T, preferred_element_type=jnp.float32) + product('tch,dch->td', qkv_back, qkv_weight)
    unit_grad = normed_grad * norm_gain
    input_grad = (inverse * (unit_grad - lax.optimization_barrier(jnp.mean(unit_grad, axis=-1, keepdims=True)) - unit_rows * lax.optimization_barrier(jnp.mean(unit_grad * unit_rows, axis=-1, keepdims=True)))).astype(jnp.bfloat16)
    return (input_grad, qkv_grad, out_grad, up_grad, down_grad)
```

```python
import math

import jax
import jax.numpy as jnp
from jax import lax
from jax.sharding import PartitionSpec as P

HEAD_DIM = 128
PATCHES = 256
EPSILON = 1e-06
F32 = jnp.float32
BF16 = jnp.bfloat16


def product(form, left_arr, right_arr):
    return jnp.einsum(form, left_arr, right_arr, preferred_element_type=F32)


def exact(form, left_arr, right_arr):
    return jnp.einsum(
        form, left_arr, right_arr, preferred_element_type=F32, precision=lax.Precision.HIGHEST
    )


def pieces(value, count):
    out = []
    for _ in range(count):
        piece = lax.reduce_precision(value, 8, 7)
        out.append(piece.astype(BF16))
        value = value - piece
    return out


def head_norm(values, gain):
    centre = jnp.mean(values, axis=-1, keepdims=True)
    centred = values - centre
    inverse = lax.rsqrt(jnp.mean(centred * centred, axis=-1, keepdims=True) + EPSILON)
    unit_rows = centred * inverse
    return (unit_rows, inverse, unit_rows * gain)


def head_norm_back(upstream, unit_rows, inverse, gain):
    scaled = upstream * gain
    return inverse * (
        scaled
        - jnp.mean(scaled, axis=-1, keepdims=True)
        - unit_rows * jnp.mean(scaled * unit_rows, axis=-1, keepdims=True)
    )


def gelu_pair(pre_act, upstream):
    hidden, pullback = jax.vjp(jax.nn.gelu, pre_act)
    return (hidden.astype(BF16), pullback(upstream)[0].astype(BF16))


def attention_pair(qkv_rows, att_grad, query_gain, key_gain):
    tok_count = qkv_rows.shape[0]
    head_width = qkv_rows.shape[2]
    head_count = head_width // HEAD_DIM
    image_count = tok_count // PATCHES
    score_scale = 1.0 / math.sqrt(HEAD_DIM)

    def per_image(values):
        return values.reshape(image_count, PATCHES, head_count, HEAD_DIM)

    query_unit, query_inverse, query_normed = head_norm(per_image(qkv_rows[:, 0]), query_gain)
    key_unit, key_inverse, key_normed = head_norm(per_image(qkv_rows[:, 1]), key_gain)
    query_normed = query_normed.astype(BF16)
    key_normed = key_normed.astype(BF16)
    value_rows = per_image(qkv_rows[:, 2]).astype(BF16)
    scores = product("ipha,iqha->ihpq", query_normed, key_normed) * score_scale
    exponent = jnp.exp(scores)
    probs = exponent / jnp.sum(exponent, axis=-1, keepdims=True)
    probs_low = probs.astype(BF16)
    attended = (
        product("ihpq,iqha->ipha", probs_low, value_rows).astype(BF16).reshape(tok_count, head_width)
    )
    grad_rows = per_image(att_grad)
    probs_grad = product("ipha,iqha->ihpq", grad_rows, value_rows)
    value_grad = product("ihpq,ipha->iqha", probs_low, grad_rows)
    score_grad = (
        probs * (probs_grad - jnp.sum(probs * probs_grad, axis=-1, keepdims=True)) * score_scale
    ).astype(BF16)
    qn_grad = product("ihpq,iqha->ipha", score_grad, key_normed)
    kn_grad = product("ihpq,ipha->iqha", score_grad, query_normed)
    query_grad = head_norm_back(qn_grad, query_unit, query_inverse, query_gain)
    key_grad = head_norm_back(kn_grad, key_unit, key_inverse, key_gain)
    qkv_back = jnp.concatenate(
        [
            query_grad.reshape(tok_count, head_width),
            key_grad.reshape(tok_count, head_width),
            value_grad.reshape(tok_count, head_width),
        ],
        axis=1,
    ).astype(BF16)
    return (attended, qkv_back)


def to_all(block, axis, count):
    rows, columns = block.shape
    spread = jnp.broadcast_to(block[None], (count, rows, columns)).reshape(count * rows, columns)
    return lax.all_to_all(spread, axis, 0, 0, tiled=True)


def local(
    hid_count,
    wid_count,
    inputs,
    cotangent,
    norm_gain,
    qkv_weight,
    out_weight,
    up_weight,
    down_weight,
    query_gain,
    key_gain,
):
    width = inputs.shape[1]
    tokens = inputs.shape[0] * hid_count
    total = float(width * wid_count)
    own = tokens // wid_count
    hidden_size = up_weight.shape[1]
    head_size = out_weight.shape[0]
    flat_qkv = qkv_weight.reshape(width, 3 * head_size)

    pre_sums = exact("d,df->f", norm_gain, up_weight.astype(F32))
    qkv_sums = exact("d,df->f", norm_gain, flat_qkv.astype(F32))
    column_sums = jnp.concatenate([pre_sums, qkv_sums])
    sum_rows = jnp.concatenate([p.reshape(-1, 128) for p in pieces(column_sums, 3)])
    sum_rows = jnp.pad(sum_rows, ((0, own - sum_rows.shape[0]), (0, 0)))

    both = to_all(jnp.concatenate([inputs, cotangent], axis=1), "hid", hid_count)
    rows, grad_all = both[:, :width].astype(F32), both[:, width:]
    part_mean = jnp.mean(rows, axis=-1, keepdims=True)
    deviation = rows - part_mean
    part_square = jnp.sum(deviation * deviation, axis=-1, keepdims=True)
    centred = (deviation * norm_gain).astype(BF16)
    stats = jnp.concatenate(pieces(part_mean, 3) + pieces(part_square, 3), axis=1)
    stats = jnp.pad(stats, ((0, 0), (0, 128 - stats.shape[1])))
    sent = jnp.concatenate(
        [
            product("td,df->tf", centred, up_weight).astype(BF16),
            product("td,df->tf", centred, flat_qkv).astype(BF16),
            product("td,fd->tf", grad_all, down_weight).astype(BF16),
            product("td,fd->tf", grad_all, out_weight).astype(BF16),
            stats,
            jnp.tile(sum_rows, (wid_count, 1)),
        ],
        axis=1,
    )
    got = lax.all_to_all(sent, "wid", 0, 0, tiled=True).reshape(wid_count, own, -1)
    edge = 2 * hidden_size + 4 * head_size
    sums = jnp.sum(got[:, :, :edge].astype(F32), axis=0)
    stats = got[:, :, edge : edge + 128].astype(F32)
    means = stats[:, :, 0] + stats[:, :, 1] + stats[:, :, 2]
    squares = stats[:, :, 3] + stats[:, :, 4] + stats[:, :, 5]
    sum_rows = got[:, :, edge + 128 :].astype(F32)
    lines = column_sums.shape[0] // 128
    all_sums = (
        sum_rows[:, :lines] + sum_rows[:, lines : 2 * lines] + sum_rows[:, 2 * lines : 3 * lines]
    ).reshape(wid_count, -1)
    mean = jnp.mean(means, axis=0)
    offset = means - mean
    variance = (jnp.sum(squares, axis=0) + float(width) * jnp.sum(offset * offset, axis=0)) / total
    inverse = lax.rsqrt(variance + EPSILON)
    normal = hidden_size + 3 * head_size
    normal_rows = inverse[:, None] * (sums[:, :normal] + exact("wt,wf->tf", offset, all_sums))
    pre_act = normal_rows[:, :hidden_size]
    hidden_grad = sums[:, normal : normal + hidden_size]
    total_sums = jnp.sum(all_sums, axis=0)
    hidden, pre_grad = gelu_pair(pre_act, hidden_grad)
    back = pre_grad.astype(F32)
    grad_sum = jnp.sum(back * total_sums[:hidden_size], axis=-1)
    grad_project = jnp.sum(back * pre_act, axis=-1)
    stats = jnp.stack(
        pieces(mean, 3) + pieces(inverse, 3) + pieces(grad_sum, 3) + pieces(grad_project, 3), axis=1
    )
    stats = jnp.pad(stats, ((0, 0), (0, 128 - stats.shape[1])))
    block = jnp.concatenate(
        [
            hidden,
            pre_grad,
            normal_rows[:, hidden_size:].astype(BF16),
            sums[:, normal + hidden_size :].astype(BF16),
            stats,
        ],
        axis=1,
    )
    shared = to_all(block, "wid", wid_count)
    hidden = shared[:, :hidden_size]
    pre_grad = shared[:, hidden_size : 2 * hidden_size]
    qkv_rows = shared[:, 2 * hidden_size : 2 * hidden_size + 3 * head_size].astype(F32)
    att_grad = shared[:, 2 * hidden_size + 3 * head_size : edge]
    stats = shared[:, edge:].astype(F32)
    mean, inverse, grad_sum, grad_project = (
        stats[:, i : i + 1] + stats[:, i + 1 : i + 2] + stats[:, i + 2 : i + 3] for i in (0, 3, 6, 9)
    )
    attended, qkv_back = attention_pair(
        qkv_rows.reshape(tokens, 3, head_size), att_grad, query_gain, key_gain
    )
    back = qkv_back.astype(F32)
    grad_sum = grad_sum + jnp.sum(back * total_sums[hidden_size:], axis=-1, keepdims=True)
    grad_project = grad_project + jnp.sum(back * qkv_rows, axis=-1, keepdims=True)
    unit_rows = (rows - mean) * inverse
    normed = (unit_rows * norm_gain).astype(BF16)
    unit_grad = norm_gain * (
        product("tf,df->td", pre_grad, up_weight) + product("tf,df->td", qkv_back, flat_qkv)
    )
    part = inverse * (unit_grad - grad_sum / total - unit_rows * (grad_project / total))
    parts = lax.all_to_all(part.astype(BF16), "hid", 0, 0, tiled=True)
    qkv_grad = product("td,tf->df", normed, qkv_back).astype(BF16)
    out_grad = product("th,td->hd", attended, grad_all).astype(BF16)
    up_grad = product("td,tf->df", normed, pre_grad).astype(BF16)
    down_grad = product("tf,td->fd", hidden, grad_all).astype(BF16)
    input_grad = jnp.sum(parts.reshape(hid_count, -1, width).astype(F32), axis=0).astype(BF16)
    return (input_grad, qkv_grad.reshape(qkv_weight.shape), out_grad, up_grad, down_grad)


def solution(mesh):
    hid_count, wid_count = mesh.shape["hid"], mesh.shape["wid"]

    def body(*args):
        return local(hid_count, wid_count, *args)

    return jax.shard_map(
        body,
        mesh=mesh,
        in_specs=(
            P("hid", "wid"),
            P("hid", "wid"),
            P("wid"),
            P("wid", None, "hid"),
            P("hid", "wid"),
            P("wid", "hid"),
            P("hid", "wid"),
            P(),
            P(),
        ),
        out_specs=(
            P("hid", "wid"),
            P("wid", None, "hid"),
            P("hid", "wid"),
            P("wid", "hid"),
            P("hid", "wid"),
        ),
        check_vma=False,
    )
```

```python
import math

import jax
import jax.numpy as jnp
from jax import lax
from jax.sharding import Mesh
from jax.sharding import PartitionSpec as P

HEAD_DIM = 128
PATCHES = 256
EPSILON = 1e-06
Z_COUNT = 16
CHIPS = 8
F32 = jnp.float32
BF16 = jnp.bfloat16


def product(form, left_arr, right_arr):
    return jnp.einsum(form, left_arr, right_arr, preferred_element_type=F32)


def exact(form, left_arr, right_arr):
    return jnp.einsum(
        form, left_arr, right_arr, preferred_element_type=F32, precision=lax.Precision.HIGHEST
    )


def pieces(value, count):
    out = []
    for _ in range(count):
        piece = lax.reduce_precision(value, 8, 7)
        out.append(piece.astype(BF16))
        value = value - piece
    return out


def head_norm(values, gain):
    centre = jnp.mean(values, axis=-1, keepdims=True)
    centred = values - centre
    inverse = lax.rsqrt(jnp.mean(centred * centred, axis=-1, keepdims=True) + EPSILON)
    unit_rows = centred * inverse
    return (unit_rows, inverse, unit_rows * gain)


def head_norm_back(upstream, unit_rows, inverse, gain):
    scaled = upstream * gain
    return inverse * (
        scaled
        - jnp.mean(scaled, axis=-1, keepdims=True)
        - unit_rows * jnp.mean(scaled * unit_rows, axis=-1, keepdims=True)
    )


def gelu_pair(pre_act, upstream):
    hidden, pullback = jax.vjp(jax.nn.gelu, pre_act)
    return (hidden.astype(BF16), pullback(upstream)[0].astype(BF16))


def attention_pair(qkv_rows, att_grad, query_gain, key_gain):
    tok_count = qkv_rows.shape[0]
    head_width = qkv_rows.shape[2]
    head_count = head_width // HEAD_DIM
    image_count = tok_count // PATCHES
    score_scale = 1.0 / math.sqrt(HEAD_DIM)

    def per_image(values):
        return values.reshape(image_count, PATCHES, head_count, HEAD_DIM)

    query_unit, query_inverse, query_normed = head_norm(per_image(qkv_rows[:, 0]), query_gain)
    key_unit, key_inverse, key_normed = head_norm(per_image(qkv_rows[:, 1]), key_gain)
    query_normed = query_normed.astype(BF16)
    key_normed = key_normed.astype(BF16)
    value_rows = per_image(qkv_rows[:, 2]).astype(BF16)
    scores = product("ipha,iqha->ihpq", query_normed, key_normed) * score_scale
    exponent = jnp.exp(scores)
    probs = exponent / jnp.sum(exponent, axis=-1, keepdims=True)
    probs_low = probs.astype(BF16)
    attended = (
        product("ihpq,iqha->ipha", probs_low, value_rows).astype(BF16).reshape(tok_count, head_width)
    )
    grad_rows = per_image(att_grad)
    probs_grad = product("ipha,iqha->ihpq", grad_rows, value_rows)
    value_grad = product("ihpq,ipha->iqha", probs_low, grad_rows)
    score_grad = (
        probs * (probs_grad - jnp.sum(probs * probs_grad, axis=-1, keepdims=True)) * score_scale
    ).astype(BF16)
    qn_grad = product("ihpq,iqha->ipha", score_grad, key_normed)
    kn_grad = product("ihpq,ipha->iqha", score_grad, query_normed)
    query_grad = head_norm_back(qn_grad, query_unit, query_inverse, query_gain)
    key_grad = head_norm_back(kn_grad, key_unit, key_inverse, key_gain)
    qkv_back = jnp.concatenate(
        [
            query_grad.reshape(tok_count, head_width),
            key_grad.reshape(tok_count, head_width),
            value_grad.reshape(tok_count, head_width),
        ],
        axis=1,
    ).astype(BF16)
    return (attended, qkv_back)


def to_all(block, axis, count):
    rows, columns = block.shape
    spread = jnp.broadcast_to(block[None], (count, rows, columns)).reshape(count * rows, columns)
    return lax.all_to_all(spread, axis, 0, 0, tiled=True)


def local(
    inputs,
    cotangent,
    norm_gain,
    qkv_weight,
    out_weight,
    up_weight,
    down_weight,
    query_gain,
    key_gain,
):
    width = inputs.shape[1]
    block = inputs.shape[0]
    total = float(width * CHIPS * 2)
    image = block * Z_COUNT
    own = image // CHIPS
    half = image // 2
    hidden_size = up_weight.shape[1]
    head_size = out_weight.shape[0]
    core = lax.axis_index("core")
    swap = [(0, 1), (1, 0)]
    flat_qkv = qkv_weight.reshape(width, 3 * head_size)

    both = to_all(jnp.concatenate([inputs, cotangent], axis=1), "z", Z_COUNT)
    own_weights = (norm_gain, up_weight, flat_qkv, down_weight, out_weight)
    other_weights = tuple(lax.ppermute(w, "core", swap) for w in own_weights)

    def column_sums(weights):
        gain, up, qkv = weights[:3]
        return jnp.concatenate(
            [exact("d,df->f", gain, up.astype(F32)), exact("d,df->f", gain, qkv.astype(F32))]
        )

    sums = column_sums(own_weights) + column_sums(other_weights)
    lines = sums.shape[0] // 128
    sum_rows = jnp.concatenate([p.reshape(-1, 128) for p in pieces(sums, 3)])
    sum_rows = jnp.pad(sum_rows, ((0, own - sum_rows.shape[0]), (0, 0)))

    low, high = both[:half], both[half:]
    pair = lax.all_to_all(
        jnp.concatenate([low, high, low, high]), ("y_lo", "core"), 0, 0, tiled=True
    ).reshape(2, 2, half, 2 * width)
    pair = jnp.swapaxes(pair, 0, 1).reshape(2, image, 2 * width)
    mine = lax.dynamic_index_in_dim(pair, core, 0, keepdims=False)
    other = lax.dynamic_index_in_dim(pair, 1 - core, 0, keepdims=False)
    rest = jnp.where(core == 0, high, low)
    rest_moved = lax.ppermute(rest, "y_lo", swap)
    y_lo = lax.axis_index("y_lo")
    rest = jnp.concatenate(
        [jnp.where(y_lo == 0, rest, rest_moved), jnp.where(y_lo == 0, rest_moved, rest)]
    )

    mine_rows, other_rows = mine[:, :width].astype(F32), other[:, :width].astype(F32)
    mine_grad, other_grad = mine[:, width:], other[:, width:]
    part_mean = (
        jnp.sum(mine_rows, axis=-1, keepdims=True) + jnp.sum(other_rows, axis=-1, keepdims=True)
    ) / float(2 * width)
    part_square = 0.0
    centred = []
    for rows, weights in ((mine_rows, own_weights), (other_rows, other_weights)):
        deviation = rows - part_mean
        part_square += jnp.sum(deviation * deviation, axis=-1, keepdims=True)
        centred.append((deviation * weights[0]).astype(BF16))
    stats = jnp.concatenate(pieces(part_mean, 3) + pieces(part_square, 3), axis=1)
    stats = jnp.pad(stats, ((0, 0), (0, 128 - stats.shape[1])))
    up_pair, qkv_pair, down_pair, out_pair = zip(own_weights[1:], other_weights[1:])

    def paired(form, left_pair, right_pair):
        return (
            product(form, left_pair[0], right_pair[0]) + product(form, left_pair[1], right_pair[1])
        ).astype(BF16)

    grads = (mine_grad, other_grad)
    sent = jnp.concatenate(
        [
            paired("td,df->tf", centred, up_pair),
            paired("td,df->tf", centred, qkv_pair),
            paired("td,fd->tf", grads, down_pair),
            paired("td,fd->tf", grads, out_pair),
            stats,
            jnp.tile(sum_rows, (CHIPS, 1)),
        ],
        axis=1,
    )
    got = lax.all_to_all(sent, ("y_hi", "x"), 0, 0, tiled=True).reshape(CHIPS, own, -1)
    edge = 2 * hidden_size + 4 * head_size
    sums = jnp.sum(got[:, :, :edge].astype(F32), axis=0)
    stats = got[:, :, edge : edge + 128].astype(F32)
    means = stats[:, :, 0] + stats[:, :, 1] + stats[:, :, 2]
    squares = stats[:, :, 3] + stats[:, :, 4] + stats[:, :, 5]
    sum_rows = got[:, :, edge + 128 :].astype(F32)
    all_sums = (
        sum_rows[:, :lines] + sum_rows[:, lines : 2 * lines] + sum_rows[:, 2 * lines : 3 * lines]
    ).reshape(CHIPS, -1)
    mean = jnp.mean(means, axis=0)
    offset = means - mean
    variance = (
        jnp.sum(squares, axis=0) + float(2 * width) * jnp.sum(offset * offset, axis=0)
    ) / total
    inverse = lax.rsqrt(variance + EPSILON)
    normal = hidden_size + 3 * head_size
    normal_rows = inverse[:, None] * (sums[:, :normal] + exact("wt,wf->tf", offset, all_sums))
    pre_act = normal_rows[:, :hidden_size]
    hidden_grad = sums[:, normal : normal + hidden_size]
    total_sums = jnp.sum(all_sums, axis=0)
    hidden, pre_grad = gelu_pair(pre_act, hidden_grad)
    back = pre_grad.astype(F32)
    grad_sum = jnp.sum(back * total_sums[:hidden_size], axis=-1)
    grad_project = jnp.sum(back * pre_act, axis=-1)
    stats = jnp.stack(
        pieces(mean, 3) + pieces(inverse, 3) + pieces(grad_sum, 3) + pieces(grad_project, 3), axis=1
    )
    stats = jnp.pad(stats, ((0, 0), (0, 128 - stats.shape[1])))
    block = jnp.concatenate(
        [
            hidden,
            pre_grad,
            normal_rows[:, hidden_size:].astype(BF16),
            sums[:, normal + hidden_size :].astype(BF16),
            stats,
        ],
        axis=1,
    )
    shared = to_all(block, ("y_hi", "x"), CHIPS)
    shared_other = lax.ppermute(shared, "core", swap)

    def unpack(shared):
        stats = shared[:, edge:].astype(F32)
        return (
            shared[:, :hidden_size],
            shared[:, hidden_size : 2 * hidden_size],
            shared[:, 2 * hidden_size : 2 * hidden_size + 3 * head_size].astype(F32),
            shared[:, 2 * hidden_size + 3 * head_size : edge],
            *(
                stats[:, i : i + 1] + stats[:, i + 1 : i + 2] + stats[:, i + 2 : i + 3]
                for i in (0, 3, 6, 9)
            ),
        )

    hidden, pre_grad, qkv_rows, att_grad, mean, inverse, grad_sum, grad_project = unpack(shared)
    attended, qkv_back = attention_pair(
        qkv_rows.reshape(image, 3, head_size), att_grad, query_gain, key_gain
    )
    attention = jnp.concatenate([attended, qkv_back], axis=1)
    attention_other = lax.ppermute(attention, "core", swap)
    back = qkv_back.astype(F32)
    grad_sum = grad_sum + jnp.sum(back * total_sums[hidden_size:], axis=-1, keepdims=True)
    grad_project = grad_project + jnp.sum(back * qkv_rows, axis=-1, keepdims=True)
    parts = []
    for rows, weights in ((mine_rows, own_weights), (other_rows, other_weights)):
        gain, up, qkv = weights[:3]
        unit_rows = (rows - mean) * inverse
        unit_grad = gain * (product("tf,df->td", pre_grad, up) + product("tf,df->td", qkv_back, qkv))
        part = inverse * (unit_grad - grad_sum / total - unit_rows * (grad_project / total))
        parts.append(part.astype(BF16).reshape(2, half, width))
    first = jnp.where(core == 0, parts[0], parts[1])
    second = jnp.where(core == 0, parts[1], parts[0])
    parts = jnp.stack([first, second], axis=1).reshape(4 * half, width)
    parts = lax.all_to_all(parts, ("y_lo", "core"), 0, 0, tiled=True).reshape(2, image, width)
    parts = jnp.sum(parts.astype(F32), axis=0).astype(BF16)
    parts = lax.all_to_all(parts, "z", 0, 0, tiled=True).reshape(Z_COUNT, -1, width)
    input_grad = jnp.sum(parts.astype(F32), axis=0).astype(BF16)

    hidden_other, pre_grad_other, _, _, mean_other, inverse_other, _, _ = unpack(shared_other)
    attended_other, back_other = attention_other[:, :head_size], attention_other[:, head_size:]
    normed = ((mine_rows - mean) * inverse * norm_gain).astype(BF16)
    normed_other = (
        (rest[:, :width].astype(F32) - mean_other) * inverse_other * norm_gain
    ).astype(BF16)
    normed = jnp.concatenate([normed, normed_other])
    grad_all = jnp.concatenate([mine_grad, rest[:, width:]])
    qkv_grad = product("td,tf->df", normed, jnp.concatenate([qkv_back, back_other])).astype(BF16)
    out_grad = product("th,td->hd", jnp.concatenate([attended, attended_other]), grad_all).astype(BF16)
    up_grad = product("td,tf->df", normed, jnp.concatenate([pre_grad, pre_grad_other])).astype(BF16)
    down_grad = product("tf,td->fd", jnp.concatenate([hidden, hidden_other]), grad_all).astype(BF16)
    return (input_grad, qkv_grad.reshape(qkv_weight.shape), out_grad, up_grad, down_grad)


def solution(mesh):
    mesh = Mesh(mesh.devices.reshape(Z_COUNT, 2, 2, 4, 2), ("z", "y_lo", "y_hi", "x", "core"))
    hid, wid = ("z", "y_lo"), ("y_hi", "x", "core")
    return jax.shard_map(
        local,
        mesh=mesh,
        in_specs=(
            P(hid, wid),
            P(hid, wid),
            P(wid),
            P(wid, None, hid),
            P(hid, wid),
            P(wid, hid),
            P(hid, wid),
            P(),
            P(),
        ),
        out_specs=(
            P(hid, wid),
            P(wid, None, hid),
            P(hid, wid),
            P(wid, hid),
            P(hid, wid),
        ),
        check_vma=False,
    )
```

```python
import functools
import math

import jax
import jax.numpy as jnp
from jax import lax
from jax.experimental import pallas as pl
from jax.experimental.pallas import tpu as pltpu
from jax.sharding import Mesh
from jax.sharding import PartitionSpec as P

HEAD_DIM = 128
PATCHES = 256
EPSILON = 1e-06
Z_COUNT = 16
CHIPS = 8
VMEM_BYTES = 24 * 1024 * 1024
F32 = jnp.float32
BF16 = jnp.bfloat16


def product(form, left_arr, right_arr):
    return jnp.einsum(form, left_arr, right_arr, preferred_element_type=F32)


def exact(form, left_arr, right_arr):
    return jnp.einsum(
        form, left_arr, right_arr, preferred_element_type=F32, precision=lax.Precision.HIGHEST
    )


def pieces(value, count):
    out = []
    for _ in range(count):
        piece = lax.reduce_precision(value, 8, 7)
        out.append(piece.astype(BF16))
        value = value - piece
    return out


def split(value, count):
    out = []
    for _ in range(count):
        piece = value.astype(BF16).astype(F32)
        out.append(piece)
        value = value - piece
    return out


def lanes(columns, rows):
    lane = lax.broadcasted_iota(jnp.int32, (rows, 128), 1)
    out = jnp.zeros((rows, 128), F32)
    for i, column in enumerate(columns):
        out = jnp.where(lane == i, column, out)
    return out.astype(BF16)


def dot(left, right, left_dim=1, right_dim=0):
    return lax.dot_general(
        left, right, (((left_dim,), (right_dim,)), ((), ())), preferred_element_type=F32
    )


def spread_kernel(inputs, cotangent, out):
    width = inputs.shape[1]
    for i in range(out.shape[0]):
        out[i, :, :width] = inputs[...]
        out[i, :, width:] = cotangent[...]


def forward_kernel(
    core,
    pair,
    own_gain,
    other_gain,
    own_up,
    other_up,
    own_qkv,
    other_qkv,
    own_down,
    other_down,
    own_out,
    other_out,
    sum_rows,
    sent,
    own_rows,
    other_rows,
):
    own_index, other_index = core[0], 1 - core[0]
    half, width = pair.shape[1], own_gain.shape[1]
    hidden_size, heads3 = own_up.shape[1], own_qkv.shape[1]
    edge = 2 * hidden_size + heads3 + own_out.shape[0]
    for y in range(2):
        at = slice(y * half, (y + 1) * half)
        own = pair[2 * y + own_index]
        other = pair[2 * y + other_index]
        own_rows[at, width:] = own[:, width:]
        other_rows[at, width:] = other[:, width:]
        own, other = own[:, :width].astype(F32), other[:, :width].astype(F32)
        part_mean = (
            jnp.sum(own, axis=1, keepdims=True) + jnp.sum(other, axis=1, keepdims=True)
        ) / float(2 * width)
        own, other = own - part_mean, other - part_mean
        part_square = jnp.sum(own * own, axis=1, keepdims=True) + jnp.sum(
            other * other, axis=1, keepdims=True
        )
        own_rows[at, :width] = (own * own_gain[...]).astype(BF16)
        other_rows[at, :width] = (other * other_gain[...]).astype(BF16)
        sent[at, edge : edge + 128] = lanes(split(part_mean, 3) + split(part_square, 3), half)
    for i in range(sent.shape[0] // sum_rows.shape[0]):
        sent[i * sum_rows.shape[0] : (i + 1) * sum_rows.shape[0], edge + 128 :] = sum_rows[...]
    start = 0
    for own_weight, other_weight, first, dim in (
        (own_up, other_up, 0, 0),
        (own_qkv, other_qkv, 0, 0),
        (own_down, other_down, width, 1),
        (own_out, other_out, width, 1),
    ):
        size = own_weight.shape[1 - dim]
        sent[:, start : start + size] = (
            dot(own_rows[:, first : first + width], own_weight[...], 1, dim)
            + dot(other_rows[:, first : first + width], other_weight[...], 1, dim)
        ).astype(BF16)
        start += size


def middle_kernel(hidden_size, width, got, block, totals):
    chips, own, _ = got.shape
    heads3 = 3 * HEAD_DIM
    normal = hidden_size + heads3
    edge = normal + hidden_size + HEAD_DIM
    lines = normal // 128
    means, squares = [], []
    for w in range(chips):
        stats = got[w, :, edge : edge + 128].astype(F32)
        means.append(stats[:, 0:1] + stats[:, 1:2] + stats[:, 2:3])
        squares.append(stats[:, 3:4] + stats[:, 4:5] + stats[:, 5:6])
    mean = sum(means) / float(chips)
    offsets = [m - mean for m in means]
    count = float(width)
    variance = (sum(squares) + count * sum(o * o for o in offsets)) / (count * chips)
    inverse = lax.rsqrt(variance + EPSILON)

    column_sums = []
    for w in range(chips):
        rows = got[w, :, edge + 128 :].astype(F32)
        column_sums.append(
            rows[:lines] + rows[lines : 2 * lines] + rows[2 * lines : 3 * lines]
        )
    total_sums = sum(column_sums)

    def summed(start):
        return sum(got[w, :, start : start + 128].astype(F32) for w in range(chips))

    def store(start, value):
        value = value.astype(BF16)
        for w in range(chips):
            block[w, :, start : start + 128] = value

    def normal_rows(line):
        value = summed(line * 128)
        for w in range(chips):
            value = value + offsets[w] * column_sums[w][line : line + 1]
        return inverse * value

    grad_sum = jnp.zeros((own, 1), F32)
    grad_project = jnp.zeros((own, 1), F32)
    scale = math.sqrt(2.0 / math.pi)
    for line in range(hidden_size // 128):
        at = line * 128
        pre_act = normal_rows(line)
        hidden_grad = summed(normal + at)
        square = pre_act * pre_act
        tanh = jnp.tanh(scale * (pre_act + 0.044715 * (square * pre_act)))
        gate = 0.5 * (1.0 + tanh)
        slope = gate + (0.5 * scale) * pre_act * (1.0 - tanh * tanh) * (1.0 + 0.134145 * square)
        pre_grad = (slope * hidden_grad).astype(BF16)
        store(at, pre_act * gate)
        store(hidden_size + at, pre_grad)
        back = pre_grad.astype(F32)
        grad_sum += jnp.sum(back * total_sums[line : line + 1], axis=1, keepdims=True)
        grad_project += jnp.sum(back * pre_act, axis=1, keepdims=True)
    for line in range(3):
        store(2 * hidden_size + line * 128, normal_rows(hidden_size // 128 + line))
    store(2 * hidden_size + heads3, summed(normal + hidden_size))
    stats = lanes(split(mean, 3) + split(inverse, 3) + split(grad_sum, 3) + split(grad_project, 3), own)
    for w in range(chips):
        block[w, :, edge:] = stats
    totals[...] = jnp.zeros(totals.shape, F32)
    totals[0:3, :] = total_sums[hidden_size // 128 :]


def head_norm(values, gain):
    centred = values - jnp.mean(values, axis=1, keepdims=True)
    inverse = lax.rsqrt(jnp.mean(centred * centred, axis=1, keepdims=True) + EPSILON)
    unit_rows = centred * inverse
    return unit_rows, inverse, (unit_rows * gain).astype(BF16)


def head_norm_back(upstream, unit_rows, inverse, gain):
    scaled = upstream * gain
    return inverse * (
        scaled
        - jnp.mean(scaled, axis=1, keepdims=True)
        - unit_rows * jnp.mean(scaled * unit_rows, axis=1, keepdims=True)
    )


def backward_kernel(
    total,
    core,
    shared,
    pair,
    own_gain,
    other_gain,
    own_up,
    other_up,
    own_qkv,
    other_qkv,
    totals,
    query_gain,
    key_gain,
    parts,
    attention,
    own_normed,
    other_normed,
):
    half, width = pair.shape[1], own_gain.shape[1]
    hidden_size = own_up.shape[1]
    start = 2 * hidden_size
    edge = start + 4 * HEAD_DIM
    score_scale = 1.0 / math.sqrt(HEAD_DIM)

    stats = shared[:, edge:].astype(F32)
    mean, inverse, grad_sum, grad_project = (
        stats[:, i : i + 1] + stats[:, i + 1 : i + 2] + stats[:, i + 2 : i + 3] for i in (0, 3, 6, 9)
    )
    query = shared[:, start : start + HEAD_DIM].astype(F32)
    key = shared[:, start + HEAD_DIM : start + 2 * HEAD_DIM].astype(F32)
    value = shared[:, start + 2 * HEAD_DIM : start + 3 * HEAD_DIM]
    att_grad = shared[:, start + 3 * HEAD_DIM : edge]
    query_unit, query_inverse, query_normed = head_norm(query, query_gain[...])
    key_unit, key_inverse, key_normed = head_norm(key, key_gain[...])
    exponent = jnp.exp(dot(query_normed, key_normed, 1, 1) * score_scale)
    probs = exponent / jnp.sum(exponent, axis=1, keepdims=True)
    probs_low = probs.astype(BF16)
    attention[:, :HEAD_DIM] = dot(probs_low, value).astype(BF16)
    probs_grad = dot(att_grad, value, 1, 1)
    value_grad = dot(probs_low, att_grad, 0, 0)
    score_grad = (
        probs * (probs_grad - jnp.sum(probs * probs_grad, axis=1, keepdims=True)) * score_scale
    ).astype(BF16)
    qn_grad = dot(score_grad, key_normed)
    kn_grad = dot(score_grad, query_normed, 0, 0)
    backs = (
        head_norm_back(qn_grad, query_unit, query_inverse, query_gain[...]),
        head_norm_back(kn_grad, key_unit, key_inverse, key_gain[...]),
        value_grad,
    )
    for i, (back, rows) in enumerate(zip(backs, (query, key, value.astype(F32)))):
        back = back.astype(BF16)
        attention[:, (i + 1) * HEAD_DIM : (i + 2) * HEAD_DIM] = back
        back = back.astype(F32)
        grad_sum += jnp.sum(back * totals[i : i + 1, :], axis=1, keepdims=True)
        grad_project += jnp.sum(back * rows, axis=1, keepdims=True)
    grad_sum, grad_project = grad_sum / total, grad_project / total
    for index, gain, up, qkv, normed in (
        (core[0], own_gain, own_up, own_qkv, own_normed),
        (1 - core[0], other_gain, other_up, other_qkv, other_normed),
    ):
        unit_grad = gain[...] * (
            dot(shared[:, hidden_size:start], up[...], 1, 1)
            + dot(attention[:, HEAD_DIM:], qkv[...], 1, 1)
        )
        for y in range(2):
            at = slice(y * half, (y + 1) * half)
            unit_rows = (pair[2 * y + index, :, :width].astype(F32) - mean[at]) * inverse[at]
            normed[at, :] = (unit_rows * gain[...]).astype(BF16)
            parts[2 * y + index] = (
                inverse[at] * (unit_grad[at] - grad_sum[at] - unit_rows * grad_project[at])
            ).astype(BF16)


def call(kernel, outs, args, scratch=(), flops=0, scalars=0):
    size = sum(math.prod(a.shape) * a.dtype.itemsize for a in (*args, *outs))
    return pl.pallas_call(
        kernel,
        out_shape=outs,
        in_specs=[pl.BlockSpec(memory_space=pltpu.SMEM)] * scalars
        + [pl.BlockSpec(memory_space=pltpu.VMEM)] * (len(args) - scalars),
        out_specs=[pl.BlockSpec(memory_space=pltpu.VMEM)] * len(outs),
        scratch_shapes=scratch,
        compiler_params=pltpu.CompilerParams(vmem_limit_bytes=VMEM_BYTES),
        cost_estimate=pl.CostEstimate(flops=flops, bytes_accessed=size, transcendentals=0),
    )(*args)


def shape(dims, dtype=BF16):
    return jax.ShapeDtypeStruct(dims, dtype)


def local(
    inputs,
    cotangent,
    norm_gain,
    qkv_weight,
    out_weight,
    up_weight,
    down_weight,
    query_gain,
    key_gain,
):
    block, width = inputs.shape
    total = float(width * CHIPS * 2)
    image = block * Z_COUNT
    own = image // CHIPS
    half = image // 2
    hidden_size = up_weight.shape[1]
    head_size = out_weight.shape[0]
    heads3 = 3 * head_size
    edge = 2 * hidden_size + heads3 + head_size
    core = lax.axis_index("core").astype(jnp.int32).reshape(1)
    swap = [(0, 1), (1, 0)]

    (spread,) = call(spread_kernel, [shape((Z_COUNT, block, 2 * width))], (inputs, cotangent))
    both = lax.all_to_all(spread.reshape(-1, 2 * width), "z", 0, 0, tiled=True)

    flat_qkv = qkv_weight.reshape(width, heads3)
    own_weights = (norm_gain.reshape(1, width), up_weight, flat_qkv, down_weight, out_weight)
    other_weights = tuple(lax.ppermute(w, "core", swap) for w in own_weights)

    def column_sums(weights):
        gain, up, qkv = weights[:3]
        return jnp.concatenate(
            [exact("d,df->f", gain[0], up.astype(F32)), exact("d,df->f", gain[0], qkv.astype(F32))]
        )

    sums = column_sums(own_weights) + column_sums(other_weights)
    sum_rows = jnp.concatenate([p.reshape(-1, 128) for p in pieces(sums, 3)])
    sum_rows = jnp.pad(sum_rows, ((0, own - sum_rows.shape[0]), (0, 0)))

    low, high = both[:half], both[half:]
    pair = lax.all_to_all(
        jnp.concatenate([low, high, low, high]), ("y_lo", "core"), 0, 0, tiled=True
    ).reshape(4, half, 2 * width)
    weight_pairs = [w for two in zip(own_weights, other_weights) for w in two]
    (sent,) = call(
        forward_kernel,
        [shape((image, edge + 256))],
        (core, pair, *weight_pairs, sum_rows),
        scratch=[pltpu.VMEM((image, 2 * width), BF16)] * 2,
        flops=4 * image * width * edge,
        scalars=1,
    )
    got = lax.all_to_all(sent, ("y_hi", "x"), 0, 0, tiled=True).reshape(CHIPS, own, -1)
    share, totals = call(
        functools.partial(middle_kernel, hidden_size, 2 * width),
        [shape((CHIPS, own, edge + 128)), shape((8, 128), F32)],
        (got,),
    )
    shared = lax.all_to_all(share.reshape(image, -1), ("y_hi", "x"), 0, 0, tiled=True)
    parts, attention, own_normed, other_normed = call(
        functools.partial(backward_kernel, total),
        [
            shape((4, half, width)),
            shape((image, 4 * head_size)),
            shape((image, width)),
            shape((image, width)),
        ],
        (
            core,
            shared,
            pair,
            *weight_pairs[:6],
            totals,
            query_gain.reshape(1, -1),
            key_gain.reshape(1, -1),
        ),
        flops=4 * image * width * (hidden_size + heads3) + 14 * image * image * head_size,
        scalars=1,
    )
    parts = lax.all_to_all(
        parts.reshape(4 * half, width), ("y_lo", "core"), 0, 0, tiled=True
    ).reshape(2, image, width)
    parts = jnp.sum(parts.astype(F32), axis=0).astype(BF16)
    parts = lax.all_to_all(parts, "z", 0, 0, tiled=True).reshape(Z_COUNT, -1, width)
    input_grad = jnp.sum(parts.astype(F32), axis=0).astype(BF16)

    hidden, pre_grad = shared[:, :hidden_size], shared[:, hidden_size : 2 * hidden_size]
    attended, qkv_back = attention[:, :head_size], attention[:, head_size:]
    by_slice = pair.reshape(2, 2, half, 2 * width)[:, :, :, width:]

    def shares(normed, index):
        grads = lax.dynamic_index_in_dim(by_slice, index, 1, keepdims=False).reshape(image, width)
        return (
            product("td,tf->df", normed, qkv_back),
            product("th,td->hd", attended, grads),
            product("td,tf->df", normed, pre_grad),
            product("tf,td->fd", hidden, grads),
        )

    moved = [lax.ppermute(s, "core", swap) for s in shares(other_normed, 1 - core[0])]
    qkv_grad, out_grad, up_grad, down_grad = (
        (mine + theirs).astype(BF16) for mine, theirs in zip(shares(own_normed, core[0]), moved)
    )
    return (input_grad, qkv_grad.reshape(qkv_weight.shape), out_grad, up_grad, down_grad)


def solution(mesh):
    mesh = Mesh(mesh.devices.reshape(Z_COUNT, 2, 2, 4, 2), ("z", "y_lo", "y_hi", "x", "core"))
    hid, wid = ("z", "y_lo"), ("y_hi", "x", "core")
    return jax.shard_map(
        local,
        mesh=mesh,
        in_specs=(
            P(hid, wid),
            P(hid, wid),
            P(wid),
            P(wid, None, hid),
            P(hid, wid),
            P(wid, hid),
            P(hid, wid),
            P(),
            P(),
        ),
        out_specs=(
            P(hid, wid),
            P(wid, None, hid),
            P(hid, wid),
            P(wid, hid),
            P(hid, wid),
        ),
        check_vma=False,
    )
```

```python
import functools
import math

import jax
import jax.numpy as jnp
from jax import lax
from jax.experimental import pallas as pl
from jax.experimental.pallas import tpu as pltpu
from jax.sharding import Mesh
from jax.sharding import PartitionSpec as P

HEAD_DIM = 128
PATCHES = 256
EPSILON = 1e-06
Z_COUNT = 16
CHIPS = 8
VMEM_BYTES = 24 * 1024 * 1024
F32 = jnp.float32
BF16 = jnp.bfloat16


def product(form, left_arr, right_arr):
    return jnp.einsum(form, left_arr, right_arr, preferred_element_type=F32)


def exact(form, left_arr, right_arr):
    return jnp.einsum(
        form, left_arr, right_arr, preferred_element_type=F32, precision=lax.Precision.HIGHEST
    )


def pieces(value, count):
    out = []
    for _ in range(count):
        piece = lax.reduce_precision(value, 8, 7)
        out.append(piece.astype(BF16))
        value = value - piece
    return out


def split(value, count):
    out = []
    for _ in range(count):
        piece = value.astype(BF16).astype(F32)
        out.append(piece)
        value = value - piece
    return out


def lanes(columns, rows):
    lane = lax.broadcasted_iota(jnp.int32, (rows, 128), 1)
    out = jnp.zeros((rows, 128), F32)
    for i, column in enumerate(columns):
        out = jnp.where(lane == i, column, out)
    return out.astype(BF16)


def dot(left, right, left_dim=1, right_dim=0):
    return lax.dot_general(
        left, right, (((left_dim,), (right_dim,)), ((), ())), preferred_element_type=F32
    )


def forward_kernel(
    core,
    pair,
    own_gain,
    other_gain,
    own_up,
    other_up,
    own_qkv,
    other_qkv,
    own_down,
    other_down,
    own_out,
    other_out,
    sum_rows,
    sent,
    own_rows,
    other_rows,
):
    own_index, other_index = core[0], 1 - core[0]
    half, width = pair.shape[1], own_gain.shape[1]
    hidden_size, heads3 = own_up.shape[1], 3 * HEAD_DIM
    edge = 2 * hidden_size + heads3 + own_out.shape[0]
    for y in range(2):
        at = slice(y * half, (y + 1) * half)
        own = pair[2 * y + own_index]
        other = pair[2 * y + other_index]
        own_rows[at, width:] = own[:, width:]
        other_rows[at, width:] = other[:, width:]
        own, other = own[:, :width].astype(F32), other[:, :width].astype(F32)
        part_mean = (
            jnp.sum(own, axis=1, keepdims=True) + jnp.sum(other, axis=1, keepdims=True)
        ) / float(2 * width)
        own, other = own - part_mean, other - part_mean
        part_square = jnp.sum(own * own, axis=1, keepdims=True) + jnp.sum(
            other * other, axis=1, keepdims=True
        )
        own_rows[at, :width] = (own * own_gain[...]).astype(BF16)
        other_rows[at, :width] = (other * other_gain[...]).astype(BF16)
        sent[at, edge : edge + 128] = lanes(split(part_mean, 3) + split(part_square, 3), half)
    for i in range(sent.shape[0] // sum_rows.shape[0]):
        sent[i * sum_rows.shape[0] : (i + 1) * sum_rows.shape[0], edge + 128 :] = sum_rows[...]
    start = 0
    for own_weight, other_weight, first, dim in (
        (own_up, other_up, 0, 0),
        *((own_qkv.at[i], other_qkv.at[i], 0, 0) for i in range(3)),
        (own_down, other_down, width, 1),
        (own_out, other_out, width, 1),
    ):
        size = own_weight.shape[1 - dim]
        sent[:, start : start + size] = (
            dot(own_rows[:, first : first + width], own_weight[...], 1, dim)
            + dot(other_rows[:, first : first + width], other_weight[...], 1, dim)
        ).astype(BF16)
        start += size


def middle_kernel(hidden_size, width, got, block, totals):
    chips, own, _ = got.shape
    heads3 = 3 * HEAD_DIM
    normal = hidden_size + heads3
    edge = normal + hidden_size + HEAD_DIM
    lines = normal // 128
    means, squares = [], []
    for w in range(chips):
        stats = got[w, :, edge : edge + 128].astype(F32)
        means.append(stats[:, 0:1] + stats[:, 1:2] + stats[:, 2:3])
        squares.append(stats[:, 3:4] + stats[:, 4:5] + stats[:, 5:6])
    mean = sum(means) / float(chips)
    offsets = [m - mean for m in means]
    count = float(width)
    variance = (sum(squares) + count * sum(o * o for o in offsets)) / (count * chips)
    inverse = lax.rsqrt(variance + EPSILON)

    column_sums = []
    for w in range(chips):
        rows = got[w, :, edge + 128 :].astype(F32)
        column_sums.append(
            rows[:lines] + rows[lines : 2 * lines] + rows[2 * lines : 3 * lines]
        )
    total_sums = sum(column_sums)

    def summed(start):
        return sum(got[w, :, start : start + 128].astype(F32) for w in range(chips))

    def store(start, value):
        value = value.astype(BF16)
        for w in range(chips):
            block[w, :, start : start + 128] = value

    def normal_rows(line):
        value = summed(line * 128)
        for w in range(chips):
            value = value + offsets[w] * column_sums[w][line : line + 1]
        return inverse * value

    grad_sum = jnp.zeros((own, 1), F32)
    grad_project = jnp.zeros((own, 1), F32)
    scale = math.sqrt(2.0 / math.pi)
    for line in range(hidden_size // 128):
        at = line * 128
        pre_act = normal_rows(line)
        hidden_grad = summed(normal + at)
        square = pre_act * pre_act
        tanh = jnp.tanh(scale * (pre_act + 0.044715 * (square * pre_act)))
        gate = 0.5 * (1.0 + tanh)
        slope = gate + (0.5 * scale) * pre_act * (1.0 - tanh * tanh) * (1.0 + 0.134145 * square)
        pre_grad = (slope * hidden_grad).astype(BF16)
        store(at, pre_act * gate)
        store(hidden_size + at, pre_grad)
        back = pre_grad.astype(F32)
        grad_sum += jnp.sum(back * total_sums[line : line + 1], axis=1, keepdims=True)
        grad_project += jnp.sum(back * pre_act, axis=1, keepdims=True)
    for line in range(3):
        store(2 * hidden_size + line * 128, normal_rows(hidden_size // 128 + line))
    store(2 * hidden_size + heads3, summed(normal + hidden_size))
    stats = lanes(split(mean, 3) + split(inverse, 3) + split(grad_sum, 3) + split(grad_project, 3), own)
    for w in range(chips):
        block[w, :, edge:] = stats
    totals[...] = jnp.zeros(totals.shape, F32)
    totals[0:3, :] = total_sums[hidden_size // 128 :]


def head_norm(values, gain):
    centred = values - jnp.mean(values, axis=1, keepdims=True)
    inverse = lax.rsqrt(jnp.mean(centred * centred, axis=1, keepdims=True) + EPSILON)
    unit_rows = centred * inverse
    return unit_rows, inverse, (unit_rows * gain).astype(BF16)


def head_norm_back(upstream, unit_rows, inverse, gain):
    scaled = upstream * gain
    return inverse * (
        scaled
        - jnp.mean(scaled, axis=1, keepdims=True)
        - unit_rows * jnp.mean(scaled * unit_rows, axis=1, keepdims=True)
    )


def backward_kernel(
    total,
    core,
    shared,
    pair,
    own_gain,
    other_gain,
    own_up,
    other_up,
    own_qkv,
    other_qkv,
    totals,
    query_gain,
    key_gain,
    parts,
    own_normed,
    bundle,
):
    half, width = pair.shape[1], own_gain.shape[1]
    hidden_size = own_up.shape[1]
    start = 2 * hidden_size
    edge = start + 4 * HEAD_DIM
    other_normed = bundle.at[:, edge : edge + width]
    attention = bundle.at[:, start:edge]
    bundle[:, :start] = shared[:, :start]
    for y in range(2):
        bundle[y * half : (y + 1) * half, edge + width :] = pair[2 * y + 1 - core[0], :, width:]
    score_scale = 1.0 / math.sqrt(HEAD_DIM)

    stats = shared[:, edge:].astype(F32)
    mean, inverse, grad_sum, grad_project = (
        stats[:, i : i + 1] + stats[:, i + 1 : i + 2] + stats[:, i + 2 : i + 3] for i in (0, 3, 6, 9)
    )
    query = shared[:, start : start + HEAD_DIM].astype(F32)
    key = shared[:, start + HEAD_DIM : start + 2 * HEAD_DIM].astype(F32)
    value = shared[:, start + 2 * HEAD_DIM : start + 3 * HEAD_DIM]
    att_grad = shared[:, start + 3 * HEAD_DIM : edge]
    query_unit, query_inverse, query_normed = head_norm(query, query_gain[...])
    key_unit, key_inverse, key_normed = head_norm(key, key_gain[...])
    exponent = jnp.exp(dot(query_normed, key_normed, 1, 1) * score_scale)
    probs = exponent / jnp.sum(exponent, axis=1, keepdims=True)
    probs_low = probs.astype(BF16)
    attention[:, :HEAD_DIM] = dot(probs_low, value).astype(BF16)
    probs_grad = dot(att_grad, value, 1, 1)
    value_grad = dot(probs_low, att_grad, 0, 0)
    score_grad = (
        probs * (probs_grad - jnp.sum(probs * probs_grad, axis=1, keepdims=True)) * score_scale
    ).astype(BF16)
    qn_grad = dot(score_grad, key_normed)
    kn_grad = dot(score_grad, query_normed, 0, 0)
    backs = (
        head_norm_back(qn_grad, query_unit, query_inverse, query_gain[...]),
        head_norm_back(kn_grad, key_unit, key_inverse, key_gain[...]),
        value_grad,
    )
    for i, (back, rows) in enumerate(zip(backs, (query, key, value.astype(F32)))):
        back = back.astype(BF16)
        attention[:, (i + 1) * HEAD_DIM : (i + 2) * HEAD_DIM] = back
        back = back.astype(F32)
        grad_sum += jnp.sum(back * totals[i : i + 1, :], axis=1, keepdims=True)
        grad_project += jnp.sum(back * rows, axis=1, keepdims=True)
    grad_sum, grad_project = grad_sum / total, grad_project / total
    for index, gain, up, qkv, normed in (
        (core[0], own_gain, own_up, own_qkv, own_normed),
        (1 - core[0], other_gain, other_up, other_qkv, other_normed),
    ):
        unit_grad = gain[...] * (
            dot(shared[:, hidden_size:start], up[...], 1, 1)
            + sum(
                dot(attention[:, (i + 1) * HEAD_DIM : (i + 2) * HEAD_DIM], qkv[i], 1, 1)
                for i in range(3)
            )
        )
        for y in range(2):
            at = slice(y * half, (y + 1) * half)
            unit_rows = (pair[2 * y + index, :, :width].astype(F32) - mean[at]) * inverse[at]
            normed[at, :] = (unit_rows * gain[...]).astype(BF16)
            parts[2 * y + index] = (
                inverse[at] * (unit_grad[at] - grad_sum[at] - unit_rows * grad_project[at])
            ).astype(BF16)


def weight_kernel(
    hidden_size, core, bundle, theirs, normed, pair, qkv_out, out_out, up_out, down_out
):
    width = normed.shape[1]
    start = 2 * hidden_size
    edge = start + 4 * HEAD_DIM
    mine = (normed[...], jnp.concatenate([pair[2 * y + core[0], :, width:] for y in range(2)]))
    other = (theirs[:, edge : edge + width], theirs[:, edge + width :])

    def both(side, first, last):
        at = slice(first, last)
        left, right = (mine[side], other[side]), (bundle[:, at], theirs[:, at])
        if side == 1:
            left, right = right, left
        return (dot(left[0], right[0], 0, 0) + dot(left[1], right[1], 0, 0)).astype(BF16)

    down_out[...] = both(1, 0, hidden_size)
    up_out[...] = both(0, hidden_size, start)
    out_out[...] = both(1, start, start + HEAD_DIM)
    qkv = both(0, start + HEAD_DIM, edge)
    for i in range(3):
        qkv_out[i] = qkv[:, i * HEAD_DIM : (i + 1) * HEAD_DIM]


def call(kernel, outs, args, scratch=(), flops=0, scalars=0):
    size = sum(math.prod(a.shape) * a.dtype.itemsize for a in (*args, *outs))
    return pl.pallas_call(
        kernel,
        out_shape=outs,
        in_specs=[pl.BlockSpec(memory_space=pltpu.SMEM)] * scalars
        + [pl.BlockSpec(memory_space=pltpu.VMEM)] * (len(args) - scalars),
        out_specs=[pl.BlockSpec(memory_space=pltpu.VMEM)] * len(outs),
        scratch_shapes=scratch,
        compiler_params=pltpu.CompilerParams(vmem_limit_bytes=VMEM_BYTES),
        cost_estimate=pl.CostEstimate(flops=flops, bytes_accessed=size, transcendentals=0),
    )(*args)


def shape(dims, dtype=BF16):
    return jax.ShapeDtypeStruct(dims, dtype)


def local(
    inputs,
    cotangent,
    norm_gain,
    qkv_weight,
    out_weight,
    up_weight,
    down_weight,
    query_gain,
    key_gain,
):
    block, width = inputs.shape
    total = float(width * CHIPS * 2)
    image = block * Z_COUNT
    own = image // CHIPS
    half = image // 2
    hidden_size = up_weight.shape[1]
    head_size = out_weight.shape[0]
    heads3 = 3 * head_size
    edge = 2 * hidden_size + heads3 + head_size
    core = lax.axis_index("core").astype(jnp.int32).reshape(1)
    swap = [(0, 1), (1, 0)]

    spread = jnp.broadcast_to(
        jnp.concatenate([inputs, cotangent], axis=1), (Z_COUNT, block, 2 * width)
    ).reshape(-1, 2 * width)
    both = lax.all_to_all(spread, "z", 0, 0, tiled=True)

    by_kind = jnp.transpose(qkv_weight, (1, 0, 2))
    own_weights = (norm_gain.reshape(1, width), up_weight, by_kind, down_weight, out_weight)
    other_weights = tuple(lax.ppermute(w, "core", swap) for w in own_weights)

    def column_sums(weights):
        gain, up, qkv = weights[:3]
        return jnp.concatenate(
            [
                exact("d,df->f", gain[0], up.astype(F32)),
                exact("d,cdj->cj", gain[0], qkv.astype(F32)).reshape(-1),
            ]
        )

    sums = column_sums(own_weights) + column_sums(other_weights)
    sum_rows = jnp.concatenate([p.reshape(-1, 128) for p in pieces(sums, 3)])
    sum_rows = jnp.pad(sum_rows, ((0, own - sum_rows.shape[0]), (0, 0)))

    low, high = both[:half], both[half:]
    pair = lax.all_to_all(
        jnp.concatenate([low, high, low, high]), ("y_lo", "core"), 0, 0, tiled=True
    ).reshape(4, half, 2 * width)
    weight_pairs = [w for two in zip(own_weights, other_weights) for w in two]
    (sent,) = call(
        forward_kernel,
        [shape((image, edge + 256))],
        (core, pair, *weight_pairs, sum_rows),
        scratch=[pltpu.VMEM((image, 2 * width), BF16)] * 2,
        flops=4 * image * width * edge,
        scalars=1,
    )
    got = lax.all_to_all(sent, ("y_hi", "x"), 0, 0, tiled=True).reshape(CHIPS, own, -1)
    share, totals = call(
        functools.partial(middle_kernel, hidden_size, 2 * width),
        [shape((CHIPS, own, edge + 128)), shape((8, 128), F32)],
        (got,),
    )
    shared = lax.all_to_all(share.reshape(image, -1), ("y_hi", "x"), 0, 0, tiled=True)
    parts, own_normed, bundle = call(
        functools.partial(backward_kernel, total),
        [
            shape((4, half, width)),
            shape((image, width)),
            shape((image, edge + 2 * width)),
        ],
        (
            core,
            shared,
            pair,
            *weight_pairs[:6],
            totals,
            query_gain.reshape(1, -1),
            key_gain.reshape(1, -1),
        ),
        flops=4 * image * width * (hidden_size + heads3) + 14 * image * image * head_size,
        scalars=1,
    )
    parts = lax.all_to_all(
        parts.reshape(4 * half, width), ("y_lo", "core"), 0, 0, tiled=True
    ).reshape(2, image, width)
    parts = jnp.sum(parts.astype(F32), axis=0).astype(BF16)
    last = lax.all_to_all(parts, "z", 0, 0, tiled=True).reshape(Z_COUNT, -1, width)

    theirs = lax.ppermute(bundle, "core", swap)
    theirs, _ = lax.optimization_barrier((theirs, parts))
    grads = call(
        functools.partial(weight_kernel, hidden_size),
        [
            shape(by_kind.shape),
            shape(out_weight.shape),
            shape(up_weight.shape),
            shape(down_weight.shape),
        ],
        (core, bundle, theirs, own_normed, pair),
        flops=4 * image * width * edge,
        scalars=1,
    )
    *grads, last = lax.optimization_barrier((*grads, last))
    input_grad = jnp.sum(last.astype(F32), axis=0).astype(BF16)
    qkv_grad, out_grad, up_grad, down_grad = grads
    return (input_grad, jnp.transpose(qkv_grad, (1, 0, 2)), out_grad, up_grad, down_grad)


def solution(mesh):
    mesh = Mesh(mesh.devices.reshape(Z_COUNT, 2, 2, 4, 2), ("z", "y_lo", "y_hi", "x", "core"))
    hid, wid = ("z", "y_lo"), ("y_hi", "x", "core")
    return jax.shard_map(
        local,
        mesh=mesh,
        in_specs=(
            P(hid, wid),
            P(hid, wid),
            P(wid),
            P(wid, None, hid),
            P(hid, wid),
            P(wid, hid),
            P(hid, wid),
            P(),
            P(),
        ),
        out_specs=(
            P(hid, wid),
            P(wid, None, hid),
            P(hid, wid),
            P(wid, hid),
            P(hid, wid),
        ),
        check_vma=False,
    )
```

```python
import functools
import math

import jax
import jax.numpy as jnp
from jax import lax
from jax.experimental import pallas as pl
from jax.experimental.pallas import tpu as pltpu
from jax.sharding import Mesh
from jax.sharding import PartitionSpec as P

HEAD_DIM = 128
PATCHES = 256
EPSILON = 1e-06
Z_COUNT = 16
CHIPS = 8
ALONG_Z = [8, 9, 10, 11, 12, 13, 14, 15, 0, 1, 2, 3, 4, 5, 6, 7]
WITHIN = [1, 0, 3, 2]
ACROSS = [6, 7, 4, 5, 2, 3, 0, 1]
VMEM_BYTES = 24 * 1024 * 1024
F32 = jnp.float32
BF16 = jnp.bfloat16


def product(form, left_arr, right_arr):
    return jnp.einsum(form, left_arr, right_arr, preferred_element_type=F32)


def exact(form, left_arr, right_arr):
    return jnp.einsum(
        form, left_arr, right_arr, preferred_element_type=F32, precision=lax.Precision.HIGHEST
    )


def pieces(value, count):
    out = []
    for _ in range(count):
        piece = lax.reduce_precision(value, 8, 7)
        out.append(piece.astype(BF16))
        value = value - piece
    return out


def split(value, count):
    out = []
    for _ in range(count):
        piece = value.astype(BF16).astype(F32)
        out.append(piece)
        value = value - piece
    return out


def lanes(columns, rows):
    lane = lax.broadcasted_iota(jnp.int32, (rows, 128), 1)
    out = jnp.zeros((rows, 128), F32)
    for i, column in enumerate(columns):
        out = jnp.where(lane == i, column, out)
    return out.astype(BF16)


def dot(left, right, left_dim=1, right_dim=0):
    return lax.dot_general(
        left, right, (((left_dim,), (right_dim,)), ((), ())), preferred_element_type=F32
    )


def forward_kernel(
    core,
    pair,
    own_gain,
    other_gain,
    own_up,
    other_up,
    own_qkv,
    other_qkv,
    own_down,
    other_down,
    own_out,
    other_out,
    sum_rows,
    sent,
    own_rows,
    other_rows,
):
    own_index, other_index = 1 - core[0], core[0]
    half, width = pair.shape[1], own_gain.shape[1]
    hidden_size, heads3 = own_up.shape[1], 3 * HEAD_DIM
    edge = 2 * hidden_size + heads3 + own_out.shape[0]
    for y in range(2):
        at = slice(y * half, (y + 1) * half)
        own = pair[2 * y + own_index]
        other = pair[2 * y + other_index]
        own_rows[at, width:] = own[:, width:]
        other_rows[at, width:] = other[:, width:]
        own, other = own[:, :width].astype(F32), other[:, :width].astype(F32)
        part_mean = (
            jnp.sum(own, axis=1, keepdims=True) + jnp.sum(other, axis=1, keepdims=True)
        ) / float(2 * width)
        own, other = own - part_mean, other - part_mean
        part_square = jnp.sum(own * own, axis=1, keepdims=True) + jnp.sum(
            other * other, axis=1, keepdims=True
        )
        own_rows[at, :width] = (own * own_gain[...]).astype(BF16)
        other_rows[at, :width] = (other * other_gain[...]).astype(BF16)
        sent[at, edge : edge + 128] = lanes(split(part_mean, 3) + split(part_square, 3), half)
    for i in range(sent.shape[0] // sum_rows.shape[0]):
        sent[i * sum_rows.shape[0] : (i + 1) * sum_rows.shape[0], edge + 128 :] = sum_rows[...]
    start = 0
    for own_weight, other_weight, first, dim in (
        (own_up, other_up, 0, 0),
        *((own_qkv.at[i], other_qkv.at[i], 0, 0) for i in range(3)),
        (own_down, other_down, width, 1),
        (own_out, other_out, width, 1),
    ):
        size = own_weight.shape[1 - dim]
        sent[:, start : start + size] = (
            dot(own_rows[:, first : first + width], own_weight[...], 1, dim)
            + dot(other_rows[:, first : first + width], other_weight[...], 1, dim)
        ).astype(BF16)
        start += size


def middle_kernel(hidden_size, width, got, block, totals):
    chips, own, _ = got.shape
    heads3 = 3 * HEAD_DIM
    normal = hidden_size + heads3
    edge = normal + hidden_size + HEAD_DIM
    lines = normal // 128
    means, squares = [], []
    for w in range(chips):
        stats = got[w, :, edge : edge + 128].astype(F32)
        means.append(stats[:, 0:1] + stats[:, 1:2] + stats[:, 2:3])
        squares.append(stats[:, 3:4] + stats[:, 4:5] + stats[:, 5:6])
    mean = sum(means) / float(chips)
    offsets = [m - mean for m in means]
    count = float(width)
    variance = (sum(squares) + count * sum(o * o for o in offsets)) / (count * chips)
    inverse = lax.rsqrt(variance + EPSILON)

    column_sums = []
    for w in range(chips):
        rows = got[w, :, edge + 128 :].astype(F32)
        column_sums.append(
            rows[:lines] + rows[lines : 2 * lines] + rows[2 * lines : 3 * lines]
        )
    total_sums = sum(column_sums)

    def summed(start):
        return sum(got[w, :, start : start + 128].astype(F32) for w in range(chips))

    def store(start, value):
        value = value.astype(BF16)
        for w in range(chips):
            block[w, :, start : start + 128] = value

    def normal_rows(line):
        value = summed(line * 128)
        for w in range(chips):
            value = value + offsets[w] * column_sums[w][line : line + 1]
        return inverse * value

    grad_sum = jnp.zeros((own, 1), F32)
    grad_project = jnp.zeros((own, 1), F32)
    scale = math.sqrt(2.0 / math.pi)
    for line in range(hidden_size // 128):
        at = line * 128
        pre_act = normal_rows(line)
        hidden_grad = summed(normal + at)
        square = pre_act * pre_act
        tanh = jnp.tanh(scale * (pre_act + 0.044715 * (square * pre_act)))
        gate = 0.5 * (1.0 + tanh)
        slope = gate + (0.5 * scale) * pre_act * (1.0 - tanh * tanh) * (1.0 + 0.134145 * square)
        pre_grad = (slope * hidden_grad).astype(BF16)
        store(at, pre_act * gate)
        store(hidden_size + at, pre_grad)
        back = pre_grad.astype(F32)
        grad_sum += jnp.sum(back * total_sums[line : line + 1], axis=1, keepdims=True)
        grad_project += jnp.sum(back * pre_act, axis=1, keepdims=True)
    for line in range(3):
        store(2 * hidden_size + line * 128, normal_rows(hidden_size // 128 + line))
    store(2 * hidden_size + heads3, summed(normal + hidden_size))
    stats = lanes(split(mean, 3) + split(inverse, 3) + split(grad_sum, 3) + split(grad_project, 3), own)
    for w in range(chips):
        block[w, :, edge:] = stats
    totals[...] = jnp.zeros(totals.shape, F32)
    totals[0:3, :] = total_sums[hidden_size // 128 :]


def head_norm(values, gain):
    centred = values - jnp.mean(values, axis=1, keepdims=True)
    inverse = lax.rsqrt(jnp.mean(centred * centred, axis=1, keepdims=True) + EPSILON)
    unit_rows = centred * inverse
    return unit_rows, inverse, (unit_rows * gain).astype(BF16)


def head_norm_back(upstream, unit_rows, inverse, gain):
    scaled = upstream * gain
    return inverse * (
        scaled
        - jnp.mean(scaled, axis=1, keepdims=True)
        - unit_rows * jnp.mean(scaled * unit_rows, axis=1, keepdims=True)
    )


def backward_kernel(
    total,
    core,
    shared,
    pair,
    own_gain,
    other_gain,
    own_up,
    other_up,
    own_qkv,
    other_qkv,
    totals,
    query_gain,
    key_gain,
    parts,
    own_normed,
    bundle,
):
    half, width = pair.shape[1], own_gain.shape[1]
    hidden_size = own_up.shape[1]
    start = 2 * hidden_size
    edge = start + 4 * HEAD_DIM
    other_normed = bundle.at[:, edge : edge + width]
    attention = bundle.at[:, start:edge]
    bundle[:, :start] = shared[:, :start]
    for y in range(2):
        bundle[y * half : (y + 1) * half, edge + width :] = pair[2 * y + core[0], :, width:]
    score_scale = 1.0 / math.sqrt(HEAD_DIM)

    stats = shared[:, edge:].astype(F32)
    mean, inverse, grad_sum, grad_project = (
        stats[:, i : i + 1] + stats[:, i + 1 : i + 2] + stats[:, i + 2 : i + 3] for i in (0, 3, 6, 9)
    )
    query = shared[:, start : start + HEAD_DIM].astype(F32)
    key = shared[:, start + HEAD_DIM : start + 2 * HEAD_DIM].astype(F32)
    value = shared[:, start + 2 * HEAD_DIM : start + 3 * HEAD_DIM]
    att_grad = shared[:, start + 3 * HEAD_DIM : edge]
    query_unit, query_inverse, query_normed = head_norm(query, query_gain[...])
    key_unit, key_inverse, key_normed = head_norm(key, key_gain[...])
    exponent = jnp.exp(dot(query_normed, key_normed, 1, 1) * score_scale)
    probs = exponent / jnp.sum(exponent, axis=1, keepdims=True)
    probs_low = probs.astype(BF16)
    attention[:, :HEAD_DIM] = dot(probs_low, value).astype(BF16)
    probs_grad = dot(att_grad, value, 1, 1)
    value_grad = dot(probs_low, att_grad, 0, 0)
    score_grad = (
        probs * (probs_grad - jnp.sum(probs * probs_grad, axis=1, keepdims=True)) * score_scale
    ).astype(BF16)
    qn_grad = dot(score_grad, key_normed)
    kn_grad = dot(score_grad, query_normed, 0, 0)
    backs = (
        head_norm_back(qn_grad, query_unit, query_inverse, query_gain[...]),
        head_norm_back(kn_grad, key_unit, key_inverse, key_gain[...]),
        value_grad,
    )
    for i, (back, rows) in enumerate(zip(backs, (query, key, value.astype(F32)))):
        back = back.astype(BF16)
        attention[:, (i + 1) * HEAD_DIM : (i + 2) * HEAD_DIM] = back
        back = back.astype(F32)
        grad_sum += jnp.sum(back * totals[i : i + 1, :], axis=1, keepdims=True)
        grad_project += jnp.sum(back * rows, axis=1, keepdims=True)
    grad_sum, grad_project = grad_sum / total, grad_project / total
    for index, gain, up, qkv, normed in (
        (1 - core[0], own_gain, own_up, own_qkv, own_normed),
        (core[0], other_gain, other_up, other_qkv, other_normed),
    ):
        unit_grad = gain[...] * (
            dot(shared[:, hidden_size:start], up[...], 1, 1)
            + sum(
                dot(attention[:, (i + 1) * HEAD_DIM : (i + 2) * HEAD_DIM], qkv[i], 1, 1)
                for i in range(3)
            )
        )
        for y in range(2):
            at = slice(y * half, (y + 1) * half)
            unit_rows = (pair[2 * y + index, :, :width].astype(F32) - mean[at]) * inverse[at]
            normed[at, :] = (unit_rows * gain[...]).astype(BF16)
            parts[2 * y + index] = (
                inverse[at] * (unit_grad[at] - grad_sum[at] - unit_rows * grad_project[at])
            ).astype(BF16)


def weight_kernel(
    hidden_size, core, bundle, theirs, normed, pair, qkv_out, out_out, up_out, down_out
):
    width = normed.shape[1]
    start = 2 * hidden_size
    edge = start + 4 * HEAD_DIM
    mine = (normed[...], jnp.concatenate([pair[2 * y + 1 - core[0], :, width:] for y in range(2)]))
    other = (theirs[:, edge : edge + width], theirs[:, edge + width :])

    def both(side, first, last):
        at = slice(first, last)
        left, right = (mine[side], other[side]), (bundle[:, at], theirs[:, at])
        if side == 1:
            left, right = right, left
        return (dot(left[0], right[0], 0, 0) + dot(left[1], right[1], 0, 0)).astype(BF16)

    down_out[...] = both(1, 0, hidden_size)
    up_out[...] = both(0, hidden_size, start)
    out_out[...] = both(1, start, start + HEAD_DIM)
    qkv = both(0, start + HEAD_DIM, edge)
    for i in range(3):
        qkv_out[i] = qkv[:, i * HEAD_DIM : (i + 1) * HEAD_DIM]


def call(kernel, outs, args, scratch=(), flops=0, scalars=0):
    size = sum(math.prod(a.shape) * a.dtype.itemsize for a in (*args, *outs))
    return pl.pallas_call(
        kernel,
        out_shape=outs,
        in_specs=[pl.BlockSpec(memory_space=pltpu.SMEM)] * scalars
        + [pl.BlockSpec(memory_space=pltpu.VMEM)] * (len(args) - scalars),
        out_specs=[pl.BlockSpec(memory_space=pltpu.VMEM)] * len(outs),
        scratch_shapes=scratch,
        compiler_params=pltpu.CompilerParams(vmem_limit_bytes=VMEM_BYTES),
        cost_estimate=pl.CostEstimate(flops=flops, bytes_accessed=size, transcendentals=0),
    )(*args)


def shape(dims, dtype=BF16):
    return jax.ShapeDtypeStruct(dims, dtype)


def to_each(rows, axis, order):
    return lax.all_to_all(rows, axis, 0, 0, tiled=True, axis_index_groups=[order])


def local(
    inputs,
    cotangent,
    norm_gain,
    qkv_weight,
    out_weight,
    up_weight,
    down_weight,
    query_gain,
    key_gain,
):
    block, width = inputs.shape
    total = float(width * CHIPS * 2)
    image = block * Z_COUNT
    own = image // CHIPS
    half = image // 2
    hidden_size = up_weight.shape[1]
    head_size = out_weight.shape[0]
    heads3 = 3 * head_size
    edge = 2 * hidden_size + heads3 + head_size
    core = lax.axis_index("core").astype(jnp.int32).reshape(1)
    swap = [(0, 1), (1, 0)]

    spread = jnp.broadcast_to(
        jnp.concatenate([inputs, cotangent], axis=1), (Z_COUNT, block, 2 * width)
    ).reshape(-1, 2 * width)
    both = to_each(spread, "z", ALONG_Z)

    by_kind = jnp.transpose(qkv_weight, (1, 0, 2))
    own_weights = (norm_gain.reshape(1, width), up_weight, by_kind, down_weight, out_weight)
    other_weights = tuple(lax.ppermute(w, "core", swap) for w in own_weights)

    def column_sums(weights):
        gain, up, qkv = weights[:3]
        return jnp.concatenate(
            [
                exact("d,df->f", gain[0], up.astype(F32)),
                exact("d,cdj->cj", gain[0], qkv.astype(F32)).reshape(-1),
            ]
        )

    sums = column_sums(own_weights) + column_sums(other_weights)
    sum_rows = jnp.concatenate([p.reshape(-1, 128) for p in pieces(sums, 3)])
    sum_rows = jnp.pad(sum_rows, ((0, own - sum_rows.shape[0]), (0, 0)))

    pair = to_each(jnp.concatenate([both, both]), ("y_lo", "core"), WITHIN)
    pair = pair.reshape(4, half, 2 * width)
    weight_pairs = [w for two in zip(own_weights, other_weights) for w in two]
    (sent,) = call(
        forward_kernel,
        [shape((image, edge + 256))],
        (core, pair, *weight_pairs, sum_rows),
        scratch=[pltpu.VMEM((image, 2 * width), BF16)] * 2,
        flops=4 * image * width * edge,
        scalars=1,
    )
    got = to_each(sent, ("y_hi", "x"), ACROSS).reshape(CHIPS, own, -1)
    share, totals = call(
        functools.partial(middle_kernel, hidden_size, 2 * width),
        [shape((CHIPS, own, edge + 128)), shape((8, 128), F32)],
        (got,),
    )
    shared = to_each(share.reshape(image, -1), ("y_hi", "x"), ACROSS)
    parts, own_normed, bundle = call(
        functools.partial(backward_kernel, total),
        [
            shape((4, half, width)),
            shape((image, width)),
            shape((image, edge + 2 * width)),
        ],
        (
            core,
            shared,
            pair,
            *weight_pairs[:6],
            totals,
            query_gain.reshape(1, -1),
            key_gain.reshape(1, -1),
        ),
        flops=4 * image * width * (hidden_size + heads3) + 14 * image * image * head_size,
        scalars=1,
    )
    parts = to_each(parts.reshape(4 * half, width), ("y_lo", "core"), WITHIN)
    parts = parts.reshape(2, image, width)
    parts = jnp.sum(parts.astype(F32), axis=0).astype(BF16)
    last = to_each(parts, "z", ALONG_Z).reshape(Z_COUNT, -1, width)

    theirs = lax.ppermute(bundle, "core", swap)
    theirs, _ = lax.optimization_barrier((theirs, parts))
    grads = call(
        functools.partial(weight_kernel, hidden_size),
        [
            shape(by_kind.shape),
            shape(out_weight.shape),
            shape(up_weight.shape),
            shape(down_weight.shape),
        ],
        (core, bundle, theirs, own_normed, pair),
        flops=4 * image * width * edge,
        scalars=1,
    )
    *grads, last = lax.optimization_barrier((*grads, last))
    input_grad = jnp.sum(last.astype(F32), axis=0).astype(BF16)
    qkv_grad, out_grad, up_grad, down_grad = grads
    return (input_grad, jnp.transpose(qkv_grad, (1, 0, 2)), out_grad, up_grad, down_grad)


def solution(mesh):
    mesh = Mesh(mesh.devices.reshape(Z_COUNT, 2, 2, 4, 2), ("z", "y_lo", "y_hi", "x", "core"))
    hid, wid = ("z", "y_lo"), ("y_hi", "x", "core")
    return jax.shard_map(
        local,
        mesh=mesh,
        in_specs=(
            P(hid, wid),
            P(hid, wid),
            P(wid),
            P(wid, None, hid),
            P(hid, wid),
            P(wid, hid),
            P(hid, wid),
            P(),
            P(),
        ),
        out_specs=(
            P(hid, wid),
            P(wid, None, hid),
            P(hid, wid),
            P(wid, hid),
            P(hid, wid),
        ),
        check_vma=False,
    )
```

```python
import functools
import math

import jax
import jax.numpy as jnp
from jax import lax
from jax.experimental import pallas as pl
from jax.experimental.pallas import tpu as pltpu
from jax.sharding import Mesh
from jax.sharding import PartitionSpec as P

HEAD_DIM = 128
PATCHES = 256
EPSILON = 1e-06
Z_COUNT = 16
CHIPS = 8
PAIRS = [4, 5, 6, 7, 0, 1, 2, 3]
NEAR = [1, 0, 3, 2, 5, 4, 7, 6]
ACROSS = [6, 7, 4, 5, 2, 3, 0, 1]
VMEM_BYTES = 24 * 1024 * 1024
F32 = jnp.float32
BF16 = jnp.bfloat16


def product(form, left_arr, right_arr):
    return jnp.einsum(form, left_arr, right_arr, preferred_element_type=F32)


def exact(form, left_arr, right_arr):
    return jnp.einsum(
        form, left_arr, right_arr, preferred_element_type=F32, precision=lax.Precision.HIGHEST
    )


def pieces(value, count):
    out = []
    for _ in range(count):
        piece = lax.reduce_precision(value, 8, 7)
        out.append(piece.astype(BF16))
        value = value - piece
    return out


def split(value, count):
    out = []
    for _ in range(count):
        piece = value.astype(BF16).astype(F32)
        out.append(piece)
        value = value - piece
    return out


def lanes(columns, rows):
    lane = lax.broadcasted_iota(jnp.int32, (rows, 128), 1)
    out = jnp.zeros((rows, 128), F32)
    for i, column in enumerate(columns):
        out = jnp.where(lane == i, column, out)
    return out.astype(BF16)


def dot(left, right, left_dim=1, right_dim=0):
    return lax.dot_general(
        left, right, (((left_dim,), (right_dim,)), ((), ())), preferred_element_type=F32
    )


def forward_kernel(
    core,
    pair,
    own_gain,
    other_gain,
    own_up,
    other_up,
    own_qkv,
    other_qkv,
    own_down,
    other_down,
    own_out,
    other_out,
    sum_rows,
    sent,
    own_rows,
    other_rows,
):
    own_index, other_index = 1 - core[0], core[0]
    part, width = pair.shape[1], own_gain.shape[1]
    hidden_size, heads3 = own_up.shape[1], 3 * HEAD_DIM
    edge = 2 * hidden_size + heads3 + own_out.shape[0]
    for i in range(4):
        at = slice(i * part, (i + 1) * part)
        own = pair[2 * i + own_index]
        other = pair[2 * i + other_index]
        own_rows[at, width:] = own[:, width:]
        other_rows[at, width:] = other[:, width:]
        own, other = own[:, :width].astype(F32), other[:, :width].astype(F32)
        part_mean = (
            jnp.sum(own, axis=1, keepdims=True) + jnp.sum(other, axis=1, keepdims=True)
        ) / float(2 * width)
        own, other = own - part_mean, other - part_mean
        part_square = jnp.sum(own * own, axis=1, keepdims=True) + jnp.sum(
            other * other, axis=1, keepdims=True
        )
        own_rows[at, :width] = (own * own_gain[...]).astype(BF16)
        other_rows[at, :width] = (other * other_gain[...]).astype(BF16)
        sent[at, edge : edge + 128] = lanes(split(part_mean, 3) + split(part_square, 3), part)
    for i in range(sent.shape[0] // sum_rows.shape[0]):
        sent[i * sum_rows.shape[0] : (i + 1) * sum_rows.shape[0], edge + 128 :] = sum_rows[...]
    start = 0
    for own_weight, other_weight, first, dim in (
        (own_up, other_up, 0, 0),
        *((own_qkv.at[i], other_qkv.at[i], 0, 0) for i in range(3)),
        (own_down, other_down, width, 1),
        (own_out, other_out, width, 1),
    ):
        size = own_weight.shape[1 - dim]
        last = own_weight.shape[0]
        sent[:, start : start + size] = (
            dot(own_rows[:, first : first + width], own_weight[...], 1, dim)
            + dot(other_rows[:, first : first + width], other_weight[:last], 1, dim)
        ).astype(BF16)
        start += size


def middle_kernel(hidden_size, width, got, block, totals):
    chips, own, _ = got.shape
    heads3 = 3 * HEAD_DIM
    normal = hidden_size + heads3
    edge = normal + hidden_size + HEAD_DIM
    lines = normal // 128
    means, squares = [], []
    for w in range(chips):
        stats = got[w, :, edge : edge + 128].astype(F32)
        means.append(stats[:, 0:1] + stats[:, 1:2] + stats[:, 2:3])
        squares.append(stats[:, 3:4] + stats[:, 4:5] + stats[:, 5:6])
    mean = sum(means) / float(chips)
    offsets = [m - mean for m in means]
    count = float(width)
    variance = (sum(squares) + count * sum(o * o for o in offsets)) / (count * chips)
    inverse = lax.rsqrt(variance + EPSILON)

    column_sums = []
    for w in range(chips):
        rows = got[w, :, edge + 128 :].astype(F32)
        column_sums.append(
            rows[:lines] + rows[lines : 2 * lines] + rows[2 * lines : 3 * lines]
        )
    total_sums = sum(column_sums)

    def summed(start):
        return sum(got[w, :, start : start + 128].astype(F32) for w in range(chips))

    def store(start, value):
        value = value.astype(BF16)
        for w in range(chips):
            block[w, :, start : start + 128] = value

    def normal_rows(line):
        value = summed(line * 128)
        for w in range(chips):
            value = value + offsets[w] * column_sums[w][line : line + 1]
        return inverse * value

    grad_sum = jnp.zeros((own, 1), F32)
    grad_project = jnp.zeros((own, 1), F32)
    scale = math.sqrt(2.0 / math.pi)
    for line in range(hidden_size // 128):
        at = line * 128
        pre_act = normal_rows(line)
        hidden_grad = summed(normal + at)
        square = pre_act * pre_act
        tanh = jnp.tanh(scale * (pre_act + 0.044715 * (square * pre_act)))
        gate = 0.5 * (1.0 + tanh)
        slope = gate + (0.5 * scale) * pre_act * (1.0 - tanh * tanh) * (1.0 + 0.134145 * square)
        pre_grad = (slope * hidden_grad).astype(BF16)
        store(at, pre_act * gate)
        store(hidden_size + at, pre_grad)
        back = pre_grad.astype(F32)
        grad_sum += jnp.sum(back * total_sums[line : line + 1], axis=1, keepdims=True)
        grad_project += jnp.sum(back * pre_act, axis=1, keepdims=True)
    for line in range(3):
        store(2 * hidden_size + line * 128, normal_rows(hidden_size // 128 + line))
    store(2 * hidden_size + heads3, summed(normal + hidden_size))
    stats = lanes(split(mean, 3) + split(inverse, 3) + split(grad_sum, 3) + split(grad_project, 3), own)
    for w in range(chips):
        block[w, :, edge:] = stats
    totals[...] = jnp.zeros(totals.shape, F32)
    totals[0:3, :] = total_sums[hidden_size // 128 :]


def head_norm(values, gain):
    centred = values - jnp.mean(values, axis=1, keepdims=True)
    inverse = lax.rsqrt(jnp.mean(centred * centred, axis=1, keepdims=True) + EPSILON)
    unit_rows = centred * inverse
    return unit_rows, inverse, (unit_rows * gain).astype(BF16)


def head_norm_back(upstream, unit_rows, inverse, gain):
    scaled = upstream * gain
    return inverse * (
        scaled
        - jnp.mean(scaled, axis=1, keepdims=True)
        - unit_rows * jnp.mean(scaled * unit_rows, axis=1, keepdims=True)
    )


def backward_kernel(
    total,
    core,
    shared,
    pair,
    own_gain,
    other_gain,
    own_up,
    other_up,
    own_qkv,
    other_qkv,
    totals,
    query_gain,
    key_gain,
    parts,
    own_normed,
    bundle,
):
    part, width = pair.shape[1], own_gain.shape[1]
    hidden_size = own_up.shape[1]
    start = 2 * hidden_size
    edge = start + 4 * HEAD_DIM
    other_normed = bundle.at[:, edge : edge + width]
    attention = bundle.at[:, start:edge]
    bundle[:, :start] = shared[:, :start]
    for i in range(4):
        bundle[i * part : (i + 1) * part, edge + width :] = pair[2 * i + core[0], :, width:]
    score_scale = 1.0 / math.sqrt(HEAD_DIM)

    stats = shared[:, edge:].astype(F32)
    mean, inverse, grad_sum, grad_project = (
        stats[:, i : i + 1] + stats[:, i + 1 : i + 2] + stats[:, i + 2 : i + 3] for i in (0, 3, 6, 9)
    )
    query = shared[:, start : start + HEAD_DIM].astype(F32)
    key = shared[:, start + HEAD_DIM : start + 2 * HEAD_DIM].astype(F32)
    value = shared[:, start + 2 * HEAD_DIM : start + 3 * HEAD_DIM]
    att_grad = shared[:, start + 3 * HEAD_DIM : edge]
    query_unit, query_inverse, query_normed = head_norm(query, query_gain[...])
    key_unit, key_inverse, key_normed = head_norm(key, key_gain[...])
    exponent = jnp.exp(dot(query_normed, key_normed, 1, 1) * score_scale)
    probs = exponent / jnp.sum(exponent, axis=1, keepdims=True)
    probs_low = probs.astype(BF16)
    attention[:, :HEAD_DIM] = dot(probs_low, value).astype(BF16)
    probs_grad = dot(att_grad, value, 1, 1)
    value_grad = dot(probs_low, att_grad, 0, 0)
    score_grad = (
        probs * (probs_grad - jnp.sum(probs * probs_grad, axis=1, keepdims=True)) * score_scale
    ).astype(BF16)
    qn_grad = dot(score_grad, key_normed)
    kn_grad = dot(score_grad, query_normed, 0, 0)
    backs = (
        head_norm_back(qn_grad, query_unit, query_inverse, query_gain[...]),
        head_norm_back(kn_grad, key_unit, key_inverse, key_gain[...]),
        value_grad,
    )
    for i, (back, rows) in enumerate(zip(backs, (query, key, value.astype(F32)))):
        back = back.astype(BF16)
        attention[:, (i + 1) * HEAD_DIM : (i + 2) * HEAD_DIM] = back
        back = back.astype(F32)
        grad_sum += jnp.sum(back * totals[i : i + 1, :], axis=1, keepdims=True)
        grad_project += jnp.sum(back * rows, axis=1, keepdims=True)
    grad_sum, grad_project = grad_sum / total, grad_project / total
    for index, gain, up, qkv, normed in (
        (1 - core[0], own_gain, own_up, own_qkv, own_normed),
        (core[0], other_gain, other_up, other_qkv, other_normed),
    ):
        unit_grad = gain[...] * (
            dot(shared[:, hidden_size:start], up[...], 1, 1)
            + sum(
                dot(attention[:, (i + 1) * HEAD_DIM : (i + 2) * HEAD_DIM], qkv[i], 1, 1)
                for i in range(3)
            )
        )
        for i in range(4):
            at = slice(i * part, (i + 1) * part)
            unit_rows = (pair[2 * i + index, :, :width].astype(F32) - mean[at]) * inverse[at]
            normed[at, :] = (unit_rows * gain[...]).astype(BF16)
            parts[2 * i + index] = (
                inverse[at] * (unit_grad[at] - grad_sum[at] - unit_rows * grad_project[at])
            ).astype(BF16)


def weight_kernel(
    hidden_size, core, bundle, theirs, normed, pair, qkv_out, out_out, up_out, down_out
):
    width = normed.shape[1]
    start = 2 * hidden_size
    edge = start + 4 * HEAD_DIM
    mine = (normed[...], jnp.concatenate([pair[2 * i + 1 - core[0], :, width:] for i in range(4)]))
    other = (theirs[:, edge : edge + width], theirs[:, edge + width :])

    def both(side, first, last):
        at = slice(first, last)
        left, right = (mine[side], other[side]), (bundle[:, at], theirs[:, at])
        if side == 1:
            left, right = right, left
        return (dot(left[0], right[0], 0, 0) + dot(left[1], right[1], 0, 0)).astype(BF16)

    down_out[...] = both(1, 0, hidden_size)
    up_out[...] = both(0, hidden_size, start)
    out_out[...] = both(1, start, start + HEAD_DIM)
    qkv = both(0, start + HEAD_DIM, edge)
    for i in range(3):
        qkv_out[i] = qkv[:, i * HEAD_DIM : (i + 1) * HEAD_DIM]


def add_kernel(parts, out):
    out[...] = sum(parts[i].astype(F32) for i in range(parts.shape[0])).astype(BF16)


def call(kernel, outs, args, scratch=(), flops=0, scalars=0):
    size = sum(math.prod(a.shape) * a.dtype.itemsize for a in (*args, *outs))
    return pl.pallas_call(
        kernel,
        out_shape=outs,
        in_specs=[pl.BlockSpec(memory_space=pltpu.SMEM)] * scalars
        + [pl.BlockSpec(memory_space=pltpu.VMEM)] * (len(args) - scalars),
        out_specs=[pl.BlockSpec(memory_space=pltpu.VMEM)] * len(outs),
        scratch_shapes=scratch,
        compiler_params=pltpu.CompilerParams(vmem_limit_bytes=VMEM_BYTES),
        cost_estimate=pl.CostEstimate(flops=flops, bytes_accessed=size, transcendentals=0),
    )(*args)


def shape(dims, dtype=BF16):
    return jax.ShapeDtypeStruct(dims, dtype)


def to_each(rows, axis, order):
    return lax.all_to_all(rows, axis, 0, 0, tiled=True, axis_index_groups=[order])


def local(
    inputs,
    cotangent,
    norm_gain,
    qkv_weight,
    out_weight,
    up_weight,
    down_weight,
    query_gain,
    key_gain,
):
    block, width = inputs.shape
    total = float(width * CHIPS * 2)
    image = block * Z_COUNT
    own = image // CHIPS
    hidden_size = up_weight.shape[1]
    head_size = out_weight.shape[0]
    heads3 = 3 * head_size
    edge = 2 * hidden_size + heads3 + head_size
    core = lax.axis_index("core").astype(jnp.int32).reshape(1)
    swap = [(0, 1), (1, 0)]

    spread = jnp.broadcast_to(
        jnp.concatenate([inputs, cotangent], axis=1), (len(PAIRS), block, 2 * width)
    ).reshape(-1, 2 * width)
    both = to_each(spread, "z_pair", PAIRS)

    by_kind = jnp.transpose(qkv_weight, (1, 0, 2))
    own_weights = (norm_gain.reshape(1, width), up_weight, by_kind, down_weight, out_weight)
    gain_rows = jnp.stack(pieces(norm_gain, 3) + [jnp.zeros((width,), BF16)] * 13)
    rows = jnp.concatenate([out_weight, gain_rows])
    other_up, other_kinds, other_down, rows = (
        lax.ppermute(w, "core", swap) for w in (up_weight, by_kind, down_weight, rows)
    )
    other_gain = jnp.sum(rows[head_size:].astype(F32), axis=0, keepdims=True)
    other_weights = (other_gain, other_up, other_kinds, other_down, rows)

    def column_sums(weights):
        gain, up, qkv = weights[:3]
        return jnp.concatenate(
            [
                exact("d,df->f", gain[0], up.astype(F32)),
                exact("d,cdj->cj", gain[0], qkv.astype(F32)).reshape(-1),
            ]
        )

    sums = column_sums(own_weights) + column_sums(other_weights)
    sum_rows = jnp.concatenate([p.reshape(-1, 128) for p in pieces(sums, 3)])
    sum_rows = jnp.pad(sum_rows, ((0, own - sum_rows.shape[0]), (0, 0)))

    pair = to_each(jnp.concatenate([both] * 4), ("z_lo", "y_lo", "core"), NEAR)
    pair = pair.reshape(8, image // 4, 2 * width)
    weight_pairs = [w for two in zip(own_weights, other_weights) for w in two]
    (sent,) = call(
        forward_kernel,
        [shape((image, edge + 256))],
        (core, pair, *weight_pairs, sum_rows),
        scratch=[pltpu.VMEM((image, 2 * width), BF16)] * 2,
        flops=4 * image * width * edge,
        scalars=1,
    )
    got = to_each(sent, ("y_hi", "x"), ACROSS).reshape(CHIPS, own, -1)
    share, totals = call(
        functools.partial(middle_kernel, hidden_size, 2 * width),
        [shape((CHIPS, own, edge + 128)), shape((8, 128), F32)],
        (got,),
    )
    shared = to_each(share.reshape(image, -1), ("y_hi", "x"), ACROSS)
    parts, own_normed, bundle = call(
        functools.partial(backward_kernel, total),
        [
            shape((8, image // 4, width)),
            shape((image, width)),
            shape((image, edge + 2 * width)),
        ],
        (
            core,
            shared,
            pair,
            *weight_pairs[:6],
            totals,
            query_gain.reshape(1, -1),
            key_gain.reshape(1, -1),
        ),
        flops=4 * image * width * (hidden_size + heads3) + 14 * image * image * head_size,
        scalars=1,
    )
    parts = to_each(parts.reshape(2 * image, width), ("z_lo", "y_lo", "core"), NEAR)
    (parts,) = call(
        add_kernel, [shape((image // 2, width))], (parts.reshape(4, image // 2, width),)
    )
    last = to_each(parts, "z_pair", PAIRS).reshape(len(PAIRS), -1, width)

    theirs = lax.ppermute(bundle, "core", swap)
    theirs, _ = lax.optimization_barrier((theirs, parts))
    grads = call(
        functools.partial(weight_kernel, hidden_size),
        [
            shape(by_kind.shape),
            shape(out_weight.shape),
            shape(up_weight.shape),
            shape(down_weight.shape),
        ],
        (core, bundle, theirs, own_normed, pair),
        flops=4 * image * width * edge,
        scalars=1,
    )
    *grads, last = lax.optimization_barrier((*grads, last))
    input_grad = jnp.sum(last.astype(F32), axis=0).astype(BF16)
    qkv_grad, out_grad, up_grad, down_grad = grads
    return (input_grad, jnp.transpose(qkv_grad, (1, 0, 2)), out_grad, up_grad, down_grad)


def solution(mesh):
    names = ("z_pair", "z_lo", "y_lo", "y_hi", "x", "core")
    mesh = Mesh(mesh.devices.reshape(Z_COUNT // 2, 2, 2, 2, 4, 2), names)
    hid, wid = names[:3], names[3:]
    return jax.shard_map(
        local,
        mesh=mesh,
        in_specs=(
            P(hid, wid),
            P(hid, wid),
            P(wid),
            P(wid, None, hid),
            P(hid, wid),
            P(wid, hid),
            P(hid, wid),
            P(),
            P(),
        ),
        out_specs=(
            P(hid, wid),
            P(wid, None, hid),
            P(hid, wid),
            P(wid, hid),
            P(hid, wid),
        ),
        check_vma=False,
    )
```

```python
import functools
import math

import jax
import jax.numpy as jnp
from jax import lax
from jax.experimental import pallas as pl
from jax.experimental.pallas import tpu as pltpu
from jax.sharding import Mesh
from jax.sharding import PartitionSpec as P

HEAD_DIM = 128
PATCHES = 256
EPSILON = 1e-06
Z_COUNT = 16
CHIPS = 8
PAIRS = [5, 6, 7, 4, 0, 1, 2, 3]
LAST = [5, 6, 7, 4, 0, 1, 2, 3]
NEAR = [1, 0, 3, 2, 5, 4, 7, 6]
ACROSS = [6, 7, 4, 5, 2, 3, 0, 1]
VMEM_BYTES = 24 * 1024 * 1024
F32 = jnp.float32
BF16 = jnp.bfloat16


def product(form, left_arr, right_arr):
    return jnp.einsum(form, left_arr, right_arr, preferred_element_type=F32)


def exact(form, left_arr, right_arr):
    return jnp.einsum(
        form, left_arr, right_arr, preferred_element_type=F32, precision=lax.Precision.HIGHEST
    )


def pieces(value, count):
    out = []
    for _ in range(count):
        piece = lax.reduce_precision(value, 8, 7)
        out.append(piece.astype(BF16))
        value = value - piece
    return out


def split(value, count):
    out = []
    for _ in range(count):
        piece = value.astype(BF16).astype(F32)
        out.append(piece)
        value = value - piece
    return out


def lanes(columns, rows):
    lane = lax.broadcasted_iota(jnp.int32, (rows, 128), 1)
    out = jnp.zeros((rows, 128), F32)
    for i, column in enumerate(columns):
        out = jnp.where(lane == i, column, out)
    return out.astype(BF16)


def dot(left, right, left_dim=1, right_dim=0):
    return lax.dot_general(
        left, right, (((left_dim,), (right_dim,)), ((), ())), preferred_element_type=F32
    )


def forward_kernel(
    core,
    pair,
    own_gain,
    other_gain,
    own_up,
    other_up,
    own_qkv,
    other_qkv,
    own_down,
    other_down,
    own_out,
    other_out,
    sum_rows,
    sent,
    own_rows,
    other_rows,
):
    own_index, other_index = 1 - core[0], core[0]
    part, width = pair.shape[1], own_gain.shape[1]
    hidden_size, heads3 = own_up.shape[1], 3 * HEAD_DIM
    edge = 2 * hidden_size + heads3 + own_out.shape[0]
    for i in range(4):
        at = slice(i * part, (i + 1) * part)
        own = pair[2 * i + own_index]
        other = pair[2 * i + other_index]
        own_rows[at, width:] = own[:, width:]
        other_rows[at, width:] = other[:, width:]
        own, other = own[:, :width].astype(F32), other[:, :width].astype(F32)
        part_mean = (
            jnp.sum(own, axis=1, keepdims=True) + jnp.sum(other, axis=1, keepdims=True)
        ) / float(2 * width)
        own, other = own - part_mean, other - part_mean
        part_square = jnp.sum(own * own, axis=1, keepdims=True) + jnp.sum(
            other * other, axis=1, keepdims=True
        )
        own_rows[at, :width] = (own * own_gain[...]).astype(BF16)
        other_rows[at, :width] = (other * other_gain[...]).astype(BF16)
        sent[at, edge : edge + 128] = lanes(split(part_mean, 3) + split(part_square, 3), part)
    for i in range(sent.shape[0] // sum_rows.shape[0]):
        sent[i * sum_rows.shape[0] : (i + 1) * sum_rows.shape[0], edge + 128 :] = sum_rows[...]
    start = 0
    for own_weight, other_weight, first, dim in (
        (own_up, other_up, 0, 0),
        *((own_qkv.at[i], other_qkv.at[i], 0, 0) for i in range(3)),
        (own_down, other_down, width, 1),
        (own_out, other_out, width, 1),
    ):
        size = own_weight.shape[1 - dim]
        last = own_weight.shape[0]
        sent[:, start : start + size] = (
            dot(own_rows[:, first : first + width], own_weight[...], 1, dim)
            + dot(other_rows[:, first : first + width], other_weight[:last], 1, dim)
        ).astype(BF16)
        start += size


def middle_kernel(hidden_size, width, got, block, totals):
    chips, own, _ = got.shape
    heads3 = 3 * HEAD_DIM
    normal = hidden_size + heads3
    edge = normal + hidden_size + HEAD_DIM
    lines = normal // 128
    means, squares = [], []
    for w in range(chips):
        stats = got[w, :, edge : edge + 128].astype(F32)
        means.append(stats[:, 0:1] + stats[:, 1:2] + stats[:, 2:3])
        squares.append(stats[:, 3:4] + stats[:, 4:5] + stats[:, 5:6])
    mean = sum(means) / float(chips)
    offsets = [m - mean for m in means]
    count = float(width)
    variance = (sum(squares) + count * sum(o * o for o in offsets)) / (count * chips)
    inverse = lax.rsqrt(variance + EPSILON)

    column_sums = []
    for w in range(chips):
        rows = got[w, :, edge + 128 :].astype(F32)
        column_sums.append(
            rows[:lines] + rows[lines : 2 * lines] + rows[2 * lines : 3 * lines]
        )
    total_sums = sum(column_sums)

    def summed(start):
        return sum(got[w, :, start : start + 128].astype(F32) for w in range(chips))

    def store(start, value):
        value = value.astype(BF16)
        for w in range(chips):
            block[w, :, start : start + 128] = value

    def normal_rows(line):
        value = summed(line * 128)
        for w in range(chips):
            value = value + offsets[w] * column_sums[w][line : line + 1]
        return inverse * value

    grad_sum = jnp.zeros((own, 1), F32)
    grad_project = jnp.zeros((own, 1), F32)
    scale = math.sqrt(2.0 / math.pi)
    for line in range(hidden_size // 128):
        at = line * 128
        pre_act = normal_rows(line)
        hidden_grad = summed(normal + at)
        square = pre_act * pre_act
        tanh = jnp.tanh(scale * (pre_act + 0.044715 * (square * pre_act)))
        gate = 0.5 * (1.0 + tanh)
        slope = gate + (0.5 * scale) * pre_act * (1.0 - tanh * tanh) * (1.0 + 0.134145 * square)
        pre_grad = (slope * hidden_grad).astype(BF16)
        store(at, pre_act * gate)
        store(hidden_size + at, pre_grad)
        back = pre_grad.astype(F32)
        grad_sum += jnp.sum(back * total_sums[line : line + 1], axis=1, keepdims=True)
        grad_project += jnp.sum(back * pre_act, axis=1, keepdims=True)
    for line in range(3):
        store(2 * hidden_size + line * 128, normal_rows(hidden_size // 128 + line))
    store(2 * hidden_size + heads3, summed(normal + hidden_size))
    stats = lanes(split(mean, 3) + split(inverse, 3) + split(grad_sum, 3) + split(grad_project, 3), own)
    for w in range(chips):
        block[w, :, edge:] = stats
    totals[...] = jnp.zeros(totals.shape, F32)
    totals[0:3, :] = total_sums[hidden_size // 128 :]


def head_norm(values, gain):
    centred = values - jnp.mean(values, axis=1, keepdims=True)
    inverse = lax.rsqrt(jnp.mean(centred * centred, axis=1, keepdims=True) + EPSILON)
    unit_rows = centred * inverse
    return unit_rows, inverse, (unit_rows * gain).astype(BF16)


def head_norm_back(upstream, unit_rows, inverse, gain):
    scaled = upstream * gain
    return inverse * (
        scaled
        - jnp.mean(scaled, axis=1, keepdims=True)
        - unit_rows * jnp.mean(scaled * unit_rows, axis=1, keepdims=True)
    )


def backward_kernel(
    total,
    core,
    shared,
    pair,
    own_gain,
    other_gain,
    own_up,
    other_up,
    own_qkv,
    other_qkv,
    totals,
    query_gain,
    key_gain,
    parts,
    own_normed,
    bundle,
):
    part, width = pair.shape[1], own_gain.shape[1]
    hidden_size = own_up.shape[1]
    start = 2 * hidden_size
    edge = start + 4 * HEAD_DIM
    other_normed = bundle.at[:, edge : edge + width]
    attention = bundle.at[:, start:edge]
    bundle[:, :start] = shared[:, :start]
    for i in range(4):
        bundle[i * part : (i + 1) * part, edge + width :] = pair[2 * i + core[0], :, width:]
    score_scale = 1.0 / math.sqrt(HEAD_DIM)

    stats = shared[:, edge:].astype(F32)
    mean, inverse, grad_sum, grad_project = (
        stats[:, i : i + 1] + stats[:, i + 1 : i + 2] + stats[:, i + 2 : i + 3] for i in (0, 3, 6, 9)
    )
    query = shared[:, start : start + HEAD_DIM].astype(F32)
    key = shared[:, start + HEAD_DIM : start + 2 * HEAD_DIM].astype(F32)
    value = shared[:, start + 2 * HEAD_DIM : start + 3 * HEAD_DIM]
    att_grad = shared[:, start + 3 * HEAD_DIM : edge]
    query_unit, query_inverse, query_normed = head_norm(query, query_gain[...])
    key_unit, key_inverse, key_normed = head_norm(key, key_gain[...])
    exponent = jnp.exp(dot(query_normed, key_normed, 1, 1) * score_scale)
    probs = exponent / jnp.sum(exponent, axis=1, keepdims=True)
    probs_low = probs.astype(BF16)
    attention[:, :HEAD_DIM] = dot(probs_low, value).astype(BF16)
    probs_grad = dot(att_grad, value, 1, 1)
    value_grad = dot(probs_low, att_grad, 0, 0)
    score_grad = (
        probs * (probs_grad - jnp.sum(probs * probs_grad, axis=1, keepdims=True)) * score_scale
    ).astype(BF16)
    qn_grad = dot(score_grad, key_normed)
    kn_grad = dot(score_grad, query_normed, 0, 0)
    backs = (
        head_norm_back(qn_grad, query_unit, query_inverse, query_gain[...]),
        head_norm_back(kn_grad, key_unit, key_inverse, key_gain[...]),
        value_grad,
    )
    for i, (back, rows) in enumerate(zip(backs, (query, key, value.astype(F32)))):
        back = back.astype(BF16)
        attention[:, (i + 1) * HEAD_DIM : (i + 2) * HEAD_DIM] = back
        back = back.astype(F32)
        grad_sum += jnp.sum(back * totals[i : i + 1, :], axis=1, keepdims=True)
        grad_project += jnp.sum(back * rows, axis=1, keepdims=True)
    grad_sum, grad_project = grad_sum / total, grad_project / total
    for index, gain, up, qkv, normed in (
        (1 - core[0], own_gain, own_up, own_qkv, own_normed),
        (core[0], other_gain, other_up, other_qkv, other_normed),
    ):
        unit_grad = gain[...] * (
            dot(shared[:, hidden_size:start], up[...], 1, 1)
            + sum(
                dot(attention[:, (i + 1) * HEAD_DIM : (i + 2) * HEAD_DIM], qkv[i], 1, 1)
                for i in range(3)
            )
        )
        for i in range(4):
            at = slice(i * part, (i + 1) * part)
            unit_rows = (pair[2 * i + index, :, :width].astype(F32) - mean[at]) * inverse[at]
            normed[at, :] = (unit_rows * gain[...]).astype(BF16)
            parts[2 * i + index] = (
                inverse[at] * (unit_grad[at] - grad_sum[at] - unit_rows * grad_project[at])
            ).astype(BF16)


def weight_kernel(
    hidden_size, core, bundle, theirs, normed, pair, qkv_out, out_out, up_out, down_out
):
    width = normed.shape[1]
    start = 2 * hidden_size
    edge = start + 4 * HEAD_DIM
    mine = (normed[...], jnp.concatenate([pair[2 * i + 1 - core[0], :, width:] for i in range(4)]))
    other = (theirs[:, edge : edge + width], theirs[:, edge + width :])

    def both(side, first, last):
        at = slice(first, last)
        left, right = (mine[side], other[side]), (bundle[:, at], theirs[:, at])
        if side == 1:
            left, right = right, left
        return (dot(left[0], right[0], 0, 0) + dot(left[1], right[1], 0, 0)).astype(BF16)

    down_out[...] = both(1, 0, hidden_size)
    up_out[...] = both(0, hidden_size, start)
    out_out[...] = both(1, start, start + HEAD_DIM)
    qkv = both(0, start + HEAD_DIM, edge)
    for i in range(3):
        qkv_out[i] = qkv[:, i * HEAD_DIM : (i + 1) * HEAD_DIM]


def add_kernel(parts, out):
    rows = out.shape[0] // len(LAST)
    for i, place in enumerate(PAIRS):
        to = LAST.index(place) * rows
        added = sum(parts[j, i * rows : (i + 1) * rows].astype(F32) for j in range(parts.shape[0]))
        out[to : to + rows] = added.astype(BF16)


def call(kernel, outs, args, scratch=(), flops=0, scalars=0):
    size = sum(math.prod(a.shape) * a.dtype.itemsize for a in (*args, *outs))
    return pl.pallas_call(
        kernel,
        out_shape=outs,
        in_specs=[pl.BlockSpec(memory_space=pltpu.SMEM)] * scalars
        + [pl.BlockSpec(memory_space=pltpu.VMEM)] * (len(args) - scalars),
        out_specs=[pl.BlockSpec(memory_space=pltpu.VMEM)] * len(outs),
        scratch_shapes=scratch,
        compiler_params=pltpu.CompilerParams(vmem_limit_bytes=VMEM_BYTES),
        cost_estimate=pl.CostEstimate(flops=flops, bytes_accessed=size, transcendentals=0),
    )(*args)


def shape(dims, dtype=BF16):
    return jax.ShapeDtypeStruct(dims, dtype)


def to_each(rows, axis, order):
    return lax.all_to_all(rows, axis, 0, 0, tiled=True, axis_index_groups=[order])


def local(
    inputs,
    cotangent,
    norm_gain,
    qkv_weight,
    out_weight,
    up_weight,
    down_weight,
    query_gain,
    key_gain,
):
    block, width = inputs.shape
    total = float(width * CHIPS * 2)
    image = block * Z_COUNT
    own = image // CHIPS
    hidden_size = up_weight.shape[1]
    head_size = out_weight.shape[0]
    heads3 = 3 * head_size
    edge = 2 * hidden_size + heads3 + head_size
    core = lax.axis_index("core").astype(jnp.int32).reshape(1)
    swap = [(0, 1), (1, 0)]

    spread = jnp.broadcast_to(
        jnp.concatenate([inputs, cotangent], axis=1), (len(PAIRS), block, 2 * width)
    ).reshape(-1, 2 * width)
    both = to_each(spread, "z_pair", PAIRS)

    by_kind = jnp.transpose(qkv_weight, (1, 0, 2))
    own_weights = (norm_gain.reshape(1, width), up_weight, by_kind, down_weight, out_weight)
    gain_rows = jnp.stack(pieces(norm_gain, 3) + [jnp.zeros((width,), BF16)] * 13)
    rows = jnp.concatenate([out_weight, gain_rows])
    other_up, other_kinds, other_down, rows = (
        lax.ppermute(w, "core", swap) for w in (up_weight, by_kind, down_weight, rows)
    )
    other_gain = jnp.sum(rows[head_size:].astype(F32), axis=0, keepdims=True)
    other_weights = (other_gain, other_up, other_kinds, other_down, rows)

    def column_sums(weights):
        gain, up, qkv = weights[:3]
        return jnp.concatenate(
            [
                exact("d,df->f", gain[0], up.astype(F32)),
                exact("d,cdj->cj", gain[0], qkv.astype(F32)).reshape(-1),
            ]
        )

    sums = column_sums(own_weights) + column_sums(other_weights)
    sum_rows = jnp.concatenate([p.reshape(-1, 128) for p in pieces(sums, 3)])
    sum_rows = jnp.pad(sum_rows, ((0, own - sum_rows.shape[0]), (0, 0)))

    pair = to_each(jnp.concatenate([both] * 4), ("z_lo", "y_lo", "core"), NEAR)
    pair = pair.reshape(8, image // 4, 2 * width)
    weight_pairs = [w for two in zip(own_weights, other_weights) for w in two]
    (sent,) = call(
        forward_kernel,
        [shape((image, edge + 256))],
        (core, pair, *weight_pairs, sum_rows),
        scratch=[pltpu.VMEM((image, 2 * width), BF16)] * 2,
        flops=4 * image * width * edge,
        scalars=1,
    )
    got = to_each(sent, ("y_hi", "x"), ACROSS).reshape(CHIPS, own, -1)
    share, totals = call(
        functools.partial(middle_kernel, hidden_size, 2 * width),
        [shape((CHIPS, own, edge + 128)), shape((8, 128), F32)],
        (got,),
    )
    shared = to_each(share.reshape(image, -1), ("y_hi", "x"), ACROSS)
    parts, own_normed, bundle = call(
        functools.partial(backward_kernel, total),
        [
            shape((8, image // 4, width)),
            shape((image, width)),
            shape((image, edge + 2 * width)),
        ],
        (
            core,
            shared,
            pair,
            *weight_pairs[:6],
            totals,
            query_gain.reshape(1, -1),
            key_gain.reshape(1, -1),
        ),
        flops=4 * image * width * (hidden_size + heads3) + 14 * image * image * head_size,
        scalars=1,
    )
    parts = to_each(parts.reshape(2 * image, width), ("z_lo", "y_lo", "core"), NEAR)
    (parts,) = call(
        add_kernel, [shape((image // 2, width))], (parts.reshape(4, image // 2, width),)
    )
    last = to_each(parts, "z_pair", LAST).reshape(len(PAIRS), -1, width)

    theirs = lax.ppermute(bundle, "core", swap)
    theirs, _ = lax.optimization_barrier((theirs, parts))
    grads = call(
        functools.partial(weight_kernel, hidden_size),
        [
            shape(by_kind.shape),
            shape(out_weight.shape),
            shape(up_weight.shape),
            shape(down_weight.shape),
        ],
        (core, bundle, theirs, own_normed, pair),
        flops=4 * image * width * edge,
        scalars=1,
    )
    *grads, last = lax.optimization_barrier((*grads, last))
    input_grad = jnp.sum(last.astype(F32), axis=0).astype(BF16)
    qkv_grad, out_grad, up_grad, down_grad = grads
    return (input_grad, jnp.transpose(qkv_grad, (1, 0, 2)), out_grad, up_grad, down_grad)


def solution(mesh):
    names = ("z_pair", "z_lo", "y_lo", "y_hi", "x", "core")
    mesh = Mesh(mesh.devices.reshape(Z_COUNT // 2, 2, 2, 2, 4, 2), names)
    hid, wid = names[:3], names[3:]
    return jax.shard_map(
        local,
        mesh=mesh,
        in_specs=(
            P(hid, wid),
            P(hid, wid),
            P(wid),
            P(wid, None, hid),
            P(hid, wid),
            P(wid, hid),
            P(hid, wid),
            P(),
            P(),
        ),
        out_specs=(
            P(hid, wid),
            P(wid, None, hid),
            P(hid, wid),
            P(wid, hid),
            P(hid, wid),
        ),
        check_vma=False,
    )
```

```python
import functools
import math

import jax
import jax.numpy as jnp
from jax import lax
from jax.experimental import pallas as pl
from jax.experimental.pallas import tpu as pltpu
from jax.sharding import Mesh
from jax.sharding import PartitionSpec as P

HEAD_DIM = 128
PATCHES = 256
EPSILON = 1e-06
Z_COUNT = 16
CHIPS = 8
PAIRS = [5, 6, 7, 4, 0, 1, 2, 3]
LAST = [5, 6, 7, 4, 0, 1, 2, 3]
NEAR = [3, 2, 1, 0, 7, 6, 5, 4]
ACROSS = [6, 7, 4, 5, 2, 3, 0, 1]
VMEM_BYTES = 24 * 1024 * 1024
F32 = jnp.float32
BF16 = jnp.bfloat16


def product(form, left_arr, right_arr):
    return jnp.einsum(form, left_arr, right_arr, preferred_element_type=F32)


def exact(form, left_arr, right_arr):
    return jnp.einsum(
        form, left_arr, right_arr, preferred_element_type=F32, precision=lax.Precision.HIGHEST
    )


def pieces(value, count):
    out = []
    for _ in range(count):
        piece = lax.reduce_precision(value, 8, 7)
        out.append(piece.astype(BF16))
        value = value - piece
    return out


def split(value, count):
    out = []
    for _ in range(count):
        piece = value.astype(BF16).astype(F32)
        out.append(piece)
        value = value - piece
    return out


def lanes(columns, rows):
    lane = lax.broadcasted_iota(jnp.int32, (rows, 128), 1)
    out = jnp.zeros((rows, 128), F32)
    for i, column in enumerate(columns):
        out = jnp.where(lane == i, column, out)
    return out.astype(BF16)


def dot(left, right, left_dim=1, right_dim=0):
    return lax.dot_general(
        left, right, (((left_dim,), (right_dim,)), ((), ())), preferred_element_type=F32
    )


def forward_kernel(
    core,
    pair,
    own_gain,
    other_gain,
    own_up,
    other_up,
    own_qkv,
    other_qkv,
    own_down,
    other_down,
    own_out,
    other_out,
    sum_rows,
    sent,
    own_rows,
    other_rows,
):
    own_index, other_index = 1 - core[0], core[0]
    part, width = pair.shape[1], own_gain.shape[1]
    hidden_size, heads3 = own_up.shape[1], 3 * HEAD_DIM
    edge = 2 * hidden_size + heads3 + own_out.shape[0]
    for i in range(4):
        at = slice(i * part, (i + 1) * part)
        own = pair[2 * i + own_index]
        other = pair[2 * i + other_index]
        own_rows[at, width:] = own[:, width:]
        other_rows[at, width:] = other[:, width:]
        own, other = own[:, :width].astype(F32), other[:, :width].astype(F32)
        part_mean = (
            jnp.sum(own, axis=1, keepdims=True) + jnp.sum(other, axis=1, keepdims=True)
        ) / float(2 * width)
        own, other = own - part_mean, other - part_mean
        part_square = jnp.sum(own * own, axis=1, keepdims=True) + jnp.sum(
            other * other, axis=1, keepdims=True
        )
        own_rows[at, :width] = (own * own_gain[...]).astype(BF16)
        other_rows[at, :width] = (other * other_gain[...]).astype(BF16)
        sent[at, edge : edge + 128] = lanes(split(part_mean, 3) + split(part_square, 3), part)
    for i in range(sent.shape[0] // sum_rows.shape[0]):
        sent[i * sum_rows.shape[0] : (i + 1) * sum_rows.shape[0], edge + 128 :] = sum_rows[...]
    start = 0
    for own_weight, other_weight, first, dim in (
        (own_up, other_up, 0, 0),
        *((own_qkv.at[i], other_qkv.at[i], 0, 0) for i in range(3)),
        (own_down, other_down, width, 1),
        (own_out, other_out, width, 1),
    ):
        size = own_weight.shape[1 - dim]
        last = own_weight.shape[0]
        sent[:, start : start + size] = (
            dot(own_rows[:, first : first + width], own_weight[...], 1, dim)
            + dot(other_rows[:, first : first + width], other_weight[:last], 1, dim)
        ).astype(BF16)
        start += size


def middle_kernel(hidden_size, width, got, block, totals):
    chips, own, _ = got.shape
    heads3 = 3 * HEAD_DIM
    normal = hidden_size + heads3
    edge = normal + hidden_size + HEAD_DIM
    lines = normal // 128
    means, squares = [], []
    for w in range(chips):
        stats = got[w, :, edge : edge + 128].astype(F32)
        means.append(stats[:, 0:1] + stats[:, 1:2] + stats[:, 2:3])
        squares.append(stats[:, 3:4] + stats[:, 4:5] + stats[:, 5:6])
    mean = sum(means) / float(chips)
    offsets = [m - mean for m in means]
    count = float(width)
    variance = (sum(squares) + count * sum(o * o for o in offsets)) / (count * chips)
    inverse = lax.rsqrt(variance + EPSILON)

    column_sums = []
    for w in range(chips):
        rows = got[w, :, edge + 128 :].astype(F32)
        column_sums.append(
            rows[:lines] + rows[lines : 2 * lines] + rows[2 * lines : 3 * lines]
        )
    total_sums = sum(column_sums)

    def summed(start):
        return sum(got[w, :, start : start + 128].astype(F32) for w in range(chips))

    def store(start, value):
        value = value.astype(BF16)
        for w in range(chips):
            block[w, :, start : start + 128] = value

    def normal_rows(line):
        value = summed(line * 128)
        for w in range(chips):
            value = value + offsets[w] * column_sums[w][line : line + 1]
        return inverse * value

    grad_sum = jnp.zeros((own, 1), F32)
    grad_project = jnp.zeros((own, 1), F32)
    scale = math.sqrt(2.0 / math.pi)
    for line in range(hidden_size // 128):
        at = line * 128
        pre_act = normal_rows(line)
        hidden_grad = summed(normal + at)
        square = pre_act * pre_act
        tanh = jnp.tanh(scale * (pre_act + 0.044715 * (square * pre_act)))
        gate = 0.5 * (1.0 + tanh)
        slope = gate + (0.5 * scale) * pre_act * (1.0 - tanh * tanh) * (1.0 + 0.134145 * square)
        pre_grad = (slope * hidden_grad).astype(BF16)
        store(at, pre_act * gate)
        store(hidden_size + at, pre_grad)
        back = pre_grad.astype(F32)
        grad_sum += jnp.sum(back * total_sums[line : line + 1], axis=1, keepdims=True)
        grad_project += jnp.sum(back * pre_act, axis=1, keepdims=True)
    for line in range(3):
        store(2 * hidden_size + line * 128, normal_rows(hidden_size // 128 + line))
    store(2 * hidden_size + heads3, summed(normal + hidden_size))
    stats = lanes(split(mean, 3) + split(inverse, 3) + split(grad_sum, 3) + split(grad_project, 3), own)
    for w in range(chips):
        block[w, :, edge:] = stats
    totals[...] = jnp.zeros(totals.shape, F32)
    totals[0:3, :] = total_sums[hidden_size // 128 :]


def head_norm(values, gain):
    centred = values - jnp.mean(values, axis=1, keepdims=True)
    inverse = lax.rsqrt(jnp.mean(centred * centred, axis=1, keepdims=True) + EPSILON)
    unit_rows = centred * inverse
    return unit_rows, inverse, (unit_rows * gain).astype(BF16)


def head_norm_back(upstream, unit_rows, inverse, gain):
    scaled = upstream * gain
    return inverse * (
        scaled
        - jnp.mean(scaled, axis=1, keepdims=True)
        - unit_rows * jnp.mean(scaled * unit_rows, axis=1, keepdims=True)
    )


def backward_kernel(
    total,
    core,
    shared,
    pair,
    own_gain,
    other_gain,
    own_up,
    other_up,
    own_qkv,
    other_qkv,
    totals,
    query_gain,
    key_gain,
    parts,
    own_normed,
    bundle,
):
    part, width = pair.shape[1], own_gain.shape[1]
    hidden_size = own_up.shape[1]
    start = 2 * hidden_size
    edge = start + 4 * HEAD_DIM
    other_normed = bundle.at[:, edge : edge + width]
    attention = bundle.at[:, start:edge]
    bundle[:, :start] = shared[:, :start]
    for i in range(4):
        bundle[i * part : (i + 1) * part, edge + width :] = pair[2 * i + core[0], :, width:]
    score_scale = 1.0 / math.sqrt(HEAD_DIM)

    stats = shared[:, edge:].astype(F32)
    mean, inverse, grad_sum, grad_project = (
        stats[:, i : i + 1] + stats[:, i + 1 : i + 2] + stats[:, i + 2 : i + 3] for i in (0, 3, 6, 9)
    )
    query = shared[:, start : start + HEAD_DIM].astype(F32)
    key = shared[:, start + HEAD_DIM : start + 2 * HEAD_DIM].astype(F32)
    value = shared[:, start + 2 * HEAD_DIM : start + 3 * HEAD_DIM]
    att_grad = shared[:, start + 3 * HEAD_DIM : edge]
    query_unit, query_inverse, query_normed = head_norm(query, query_gain[...])
    key_unit, key_inverse, key_normed = head_norm(key, key_gain[...])
    exponent = jnp.exp(dot(query_normed, key_normed, 1, 1) * score_scale)
    probs = exponent / jnp.sum(exponent, axis=1, keepdims=True)
    probs_low = probs.astype(BF16)
    attention[:, :HEAD_DIM] = dot(probs_low, value).astype(BF16)
    probs_grad = dot(att_grad, value, 1, 1)
    value_grad = dot(probs_low, att_grad, 0, 0)
    score_grad = (
        probs * (probs_grad - jnp.sum(probs * probs_grad, axis=1, keepdims=True)) * score_scale
    ).astype(BF16)
    qn_grad = dot(score_grad, key_normed)
    kn_grad = dot(score_grad, query_normed, 0, 0)
    backs = (
        head_norm_back(qn_grad, query_unit, query_inverse, query_gain[...]),
        head_norm_back(kn_grad, key_unit, key_inverse, key_gain[...]),
        value_grad,
    )
    for i, (back, rows) in enumerate(zip(backs, (query, key, value.astype(F32)))):
        back = back.astype(BF16)
        attention[:, (i + 1) * HEAD_DIM : (i + 2) * HEAD_DIM] = back
        back = back.astype(F32)
        grad_sum += jnp.sum(back * totals[i : i + 1, :], axis=1, keepdims=True)
        grad_project += jnp.sum(back * rows, axis=1, keepdims=True)
    grad_sum, grad_project = grad_sum / total, grad_project / total
    for index, gain, up, qkv, normed in (
        (1 - core[0], own_gain, own_up, own_qkv, own_normed),
        (core[0], other_gain, other_up, other_qkv, other_normed),
    ):
        unit_grad = gain[...] * (
            dot(shared[:, hidden_size:start], up[...], 1, 1)
            + sum(
                dot(attention[:, (i + 1) * HEAD_DIM : (i + 2) * HEAD_DIM], qkv[i], 1, 1)
                for i in range(3)
            )
        )
        for i in range(4):
            at = slice(i * part, (i + 1) * part)
            unit_rows = (pair[2 * i + index, :, :width].astype(F32) - mean[at]) * inverse[at]
            normed[at, :] = (unit_rows * gain[...]).astype(BF16)
            parts[2 * i + index] = (
                inverse[at] * (unit_grad[at] - grad_sum[at] - unit_rows * grad_project[at])
            ).astype(BF16)


def weight_kernel(
    hidden_size, core, bundle, theirs, normed, pair, qkv_out, out_out, up_out, down_out
):
    width = normed.shape[1]
    start = 2 * hidden_size
    edge = start + 4 * HEAD_DIM
    mine = (normed[...], jnp.concatenate([pair[2 * i + 1 - core[0], :, width:] for i in range(4)]))
    other = (theirs[:, edge : edge + width], theirs[:, edge + width :])

    def both(side, first, last):
        at = slice(first, last)
        left, right = (mine[side], other[side]), (bundle[:, at], theirs[:, at])
        if side == 1:
            left, right = right, left
        return (dot(left[0], right[0], 0, 0) + dot(left[1], right[1], 0, 0)).astype(BF16)

    down_out[...] = both(1, 0, hidden_size)
    up_out[...] = both(0, hidden_size, start)
    out_out[...] = both(1, start, start + HEAD_DIM)
    qkv = both(0, start + HEAD_DIM, edge)
    for i in range(3):
        qkv_out[i] = qkv[:, i * HEAD_DIM : (i + 1) * HEAD_DIM]


def add_kernel(parts, out):
    rows = out.shape[0] // len(LAST)
    for i, place in enumerate(PAIRS):
        to = LAST.index(place) * rows
        added = sum(parts[j, i * rows : (i + 1) * rows].astype(F32) for j in range(parts.shape[0]))
        out[to : to + rows] = added.astype(BF16)


def call(kernel, outs, args, scratch=(), flops=0, scalars=0):
    size = sum(math.prod(a.shape) * a.dtype.itemsize for a in (*args, *outs))
    return pl.pallas_call(
        kernel,
        out_shape=outs,
        in_specs=[pl.BlockSpec(memory_space=pltpu.SMEM)] * scalars
        + [pl.BlockSpec(memory_space=pltpu.VMEM)] * (len(args) - scalars),
        out_specs=[pl.BlockSpec(memory_space=pltpu.VMEM)] * len(outs),
        scratch_shapes=scratch,
        compiler_params=pltpu.CompilerParams(vmem_limit_bytes=VMEM_BYTES),
        cost_estimate=pl.CostEstimate(flops=flops, bytes_accessed=size, transcendentals=0),
    )(*args)


def shape(dims, dtype=BF16):
    return jax.ShapeDtypeStruct(dims, dtype)


def to_each(rows, axis, order):
    return lax.all_to_all(rows, axis, 0, 0, tiled=True, axis_index_groups=[order])


def local(
    inputs,
    cotangent,
    norm_gain,
    qkv_weight,
    out_weight,
    up_weight,
    down_weight,
    query_gain,
    key_gain,
):
    block, width = inputs.shape
    total = float(width * CHIPS * 2)
    image = block * Z_COUNT
    own = image // CHIPS
    hidden_size = up_weight.shape[1]
    head_size = out_weight.shape[0]
    heads3 = 3 * head_size
    edge = 2 * hidden_size + heads3 + head_size
    core = lax.axis_index("core").astype(jnp.int32).reshape(1)
    swap = [(0, 1), (1, 0)]

    spread = jnp.broadcast_to(
        jnp.concatenate([inputs, cotangent], axis=1), (len(PAIRS), block, 2 * width)
    ).reshape(-1, 2 * width)
    both = to_each(spread, "z_pair", PAIRS)

    by_kind = jnp.transpose(qkv_weight, (1, 0, 2))
    own_weights = (norm_gain.reshape(1, width), up_weight, by_kind, down_weight, out_weight)
    gain_rows = jnp.stack(pieces(norm_gain, 3) + [jnp.zeros((width,), BF16)] * 13)
    rows = jnp.concatenate([out_weight, gain_rows])
    other_up, other_kinds, other_down, rows = (
        lax.ppermute(w, "core", swap) for w in (up_weight, by_kind, down_weight, rows)
    )
    other_gain = jnp.sum(rows[head_size:].astype(F32), axis=0, keepdims=True)
    other_weights = (other_gain, other_up, other_kinds, other_down, rows)

    def column_sums(weights):
        gain, up, qkv = weights[:3]
        return jnp.concatenate(
            [
                exact("d,df->f", gain[0], up.astype(F32)),
                exact("d,cdj->cj", gain[0], qkv.astype(F32)).reshape(-1),
            ]
        )

    sums = column_sums(own_weights) + column_sums(other_weights)
    sum_rows = jnp.concatenate([p.reshape(-1, 128) for p in pieces(sums, 3)])
    sum_rows = jnp.pad(sum_rows, ((0, own - sum_rows.shape[0]), (0, 0)))

    pair = to_each(jnp.concatenate([both] * 4), ("z_lo", "y_lo", "core"), NEAR)
    pair = pair.reshape(8, image // 4, 2 * width)
    weight_pairs = [w for two in zip(own_weights, other_weights) for w in two]
    (sent,) = call(
        forward_kernel,
        [shape((image, edge + 256))],
        (core, pair, *weight_pairs, sum_rows),
        scratch=[pltpu.VMEM((image, 2 * width), BF16)] * 2,
        flops=4 * image * width * edge,
        scalars=1,
    )
    got = to_each(sent, ("y_hi", "x"), ACROSS).reshape(CHIPS, own, -1)
    share, totals = call(
        functools.partial(middle_kernel, hidden_size, 2 * width),
        [shape((CHIPS, own, edge + 128)), shape((8, 128), F32)],
        (got,),
    )
    shared = to_each(share.reshape(image, -1), ("y_hi", "x"), ACROSS)
    parts, own_normed, bundle = call(
        functools.partial(backward_kernel, total),
        [
            shape((8, image // 4, width)),
            shape((image, width)),
            shape((image, edge + 2 * width)),
        ],
        (
            core,
            shared,
            pair,
            *weight_pairs[:6],
            totals,
            query_gain.reshape(1, -1),
            key_gain.reshape(1, -1),
        ),
        flops=4 * image * width * (hidden_size + heads3) + 14 * image * image * head_size,
        scalars=1,
    )
    parts = to_each(parts.reshape(2 * image, width), ("z_lo", "y_lo", "core"), NEAR)
    (parts,) = call(
        add_kernel, [shape((image // 2, width))], (parts.reshape(4, image // 2, width),)
    )
    last = to_each(parts, "z_pair", LAST).reshape(len(PAIRS), -1, width)

    theirs = lax.ppermute(bundle, "core", swap)
    theirs, _ = lax.optimization_barrier((theirs, parts))
    grads = call(
        functools.partial(weight_kernel, hidden_size),
        [
            shape(by_kind.shape),
            shape(out_weight.shape),
            shape(up_weight.shape),
            shape(down_weight.shape),
        ],
        (core, bundle, theirs, own_normed, pair),
        flops=4 * image * width * edge,
        scalars=1,
    )
    *grads, last = lax.optimization_barrier((*grads, last))
    input_grad = jnp.sum(last.astype(F32), axis=0).astype(BF16)
    qkv_grad, out_grad, up_grad, down_grad = grads
    return (input_grad, jnp.transpose(qkv_grad, (1, 0, 2)), out_grad, up_grad, down_grad)


def solution(mesh):
    names = ("z_pair", "z_lo", "y_lo", "y_hi", "x", "core")
    mesh = Mesh(mesh.devices.reshape(Z_COUNT // 2, 2, 2, 2, 4, 2), names)
    hid, wid = names[:3], names[3:]
    return jax.shard_map(
        local,
        mesh=mesh,
        in_specs=(
            P(hid, wid),
            P(hid, wid),
            P(wid),
            P(wid, None, hid),
            P(hid, wid),
            P(wid, hid),
            P(hid, wid),
            P(),
            P(),
        ),
        out_specs=(
            P(hid, wid),
            P(wid, None, hid),
            P(hid, wid),
            P(wid, hid),
            P(hid, wid),
        ),
        check_vma=False,
    )
```
